32 devices in a mesh: rad: 4 (over y, core), azi: 8 (over z, x).
Axes of the slice: x: 2, y: 2, z: 4, core: 2. Of those that a mesh axis runs over, the one named last changes fastest.
Arguments:
- fields: float32 [5, 8, 512, 512], P(None, None, 'azi', 'rad'), may hold values from -6 to 6
- radial_metric: float32 [512], P('rad'), may hold values from 0.5 to 2
- azimuth_metric: float32 [512], P('rad'), may hold values from 0.5 to 2
Outputs:
- grad_azimuth: float32 [5, 8, 512, 512], P(None, None, 'azi', 'rad')
- grad_radial: float32 [5, 8, 512, 512], P(None, None, 'azi', 'rad')
- filtered: float32 [5, 8, 512, 512], P(None, None, 'azi', 'rad')
The draws below stay inside these ranges and needn't reach their ends.
All inputs are finite; a program needn't handle non-finite values.
Results may differ from the reference program's by a relative error of at most 0.0003.
Values sent between devices are 32-bit elements; how exact they have to be, the bound alone decides.
A program may use at most 192 MiB of HBM per device.

```python
import math
import jax
import jax.numpy as jnp
from jax import lax

NF = 5
AX = 8
NT = 512
NR = 512


def levels(rng, extent, shards, smallest, top_value):
    def one(dim, blocks):
        heights = jax.random.uniform(jax.random.fold_in(jax.random.fold_in(rng, 6), dim), (blocks,), jnp.float32, smallest / len(shards), top_value / len(shards))
        return jnp.repeat(jnp.exp(heights), extent[dim] // blocks).reshape((-1,) + (1,) * (len(extent) - dim - 1))

    loudness = one(*shards[0])
    for cut in shards[1:]:
        loudness = loudness * one(*cut)
    return loudness


def normal_values(rng, shape, scale, bound, cuts=(), kind=jnp.bfloat16):
    values = jax.random.normal(rng, shape, jnp.float32) * scale
    if len(cuts) > 0:
        values = levels(rng, shape, cuts, -0.22, 0.18) * values
    return jnp.clip(values, min=-bound, max=bound).astype(kind)


def setup_inputs(seed: int = 0) -> dict:
    keys = jax.random.split(jax.random.key(seed), 4)
    return {
        "fields": normal_values(keys[0], (NF, AX, NT, NR), 1.0, 6.0, ((2, 8), (3, 4)), jnp.float32),
        "radial_metric": jnp.clip(jnp.exp(math.log(2.0) - 1.3862944 * jax.random.uniform(keys[1], (NR,), jnp.float32) ** levels(keys[1], (NR,), ((0, 4),), -0.2, 0.2)), 0.5, 2.0),
        "azimuth_metric": jnp.clip(jnp.exp(math.log(2.0) - 1.3862944 * jax.random.uniform(keys[2], (NR,), jnp.float32) ** levels(keys[2], (NR,), ((0, 4),), -0.2, 0.2)), 0.5, 2.0),
    }


ALPHA_D = 1.0 / 3.0
COEF_A = 14.0 / 9.0
COEF_B = 1.0 / 9.0
ALPHA_F = 0.49

def filter_weights():
    slack = 1.0 - 2.0 * ALPHA_F
    return [(193.0 + 126.0 * ALPHA_F) / 256.0, (105.0 + 302.0 * ALPHA_F) / 256.0, -15.0 * slack / 64.0, 45.0 * slack / 512.0, -5.0 * slack / 256.0, slack / 512.0]

def periodic_solve(source, alpha):
    count = source.shape[1]
    waves = jnp.arange(count).astype(source.dtype)
    symbol = 1.0 + 2.0 * alpha * jnp.cos(2.0 * jnp.pi * waves / count)
    spectrum = jnp.fft.fft(source, axis=1) / symbol[:, None]
    return jnp.real(jnp.fft.ifft(spectrum, axis=1)).astype(source.dtype)

def one_field(field):

    def along(offset):
        return jnp.roll(field, -offset, axis=1)
    slope_side = 0.5 * COEF_A * (along(1) - along(-1)) + 0.25 * COEF_B * (along(2) - along(-2))
    weights = filter_weights()
    smooth_side = weights[0] * field
    for offset in range(1, 6):
        smooth_side = smooth_side + 0.5 * weights[offset] * (along(offset) + along(-offset))
    slope_azi = periodic_solve(slope_side, ALPHA_D)
    smoothed = periodic_solve(smooth_side, ALPHA_F)
    count = field.shape[2]
    padded = jnp.pad(field, ((0, 0), (0, 0), (2, 2)))

    def radial(offset):
        return padded[:, :, 2 + offset:2 + offset + count]
    radial_side = 0.5 * COEF_A * (radial(1) - radial(-1)) + 0.25 * COEF_B * (radial(2) - radial(-2))
    flat = radial_side.reshape(-1, count).T
    lower = jnp.full((count,), ALPHA_D, field.dtype).at[0].set(0.0)
    upper = jnp.full((count,), ALPHA_D, field.dtype).at[count - 1].set(0.0)
    middle = jnp.ones((count,), field.dtype)
    solved = lax.linalg.tridiagonal_solve(lower, middle, upper, flat)
    slope_rad = solved.T.reshape(field.shape)
    return (slope_azi, slope_rad, smoothed)

def reference(fields, radial_metric, azimuth_metric):
    slope_azi, slope_rad, smoothed = lax.map(one_field, fields)
    return (slope_azi * azimuth_metric, slope_rad * radial_metric, smoothed)
```

```python
import functools

import jax
import jax.numpy as jnp
import ml_dtypes
import numpy as np
from jax import lax
from jax.experimental import pallas as pl
from jax.experimental.pallas import tpu as pltpu
from jax.sharding import PartitionSpec as P

ALPHA_D = 1.0 / 3.0
COEF_A = 14.0 / 9.0
COEF_B = 1.0 / 9.0
ALPHA_F = 0.49
MESH = pl.DeviceIdType.MESH
BF16 = jnp.bfloat16
F32 = jnp.float32

RAW = 4
SUMS = 2
PACK = 4


def filter_weights():
    slack = 1.0 - 2.0 * ALPHA_F
    return [
        (193.0 + 126.0 * ALPHA_F) / 256.0,
        (105.0 + 302.0 * ALPHA_F) / 256.0,
        -15.0 * slack / 64.0,
        45.0 * slack / 512.0,
        -5.0 * slack / 256.0,
        slack / 512.0,
    ]


def split(table):
    table = np.asarray(table, np.float32)
    high = table.astype(ml_dtypes.bfloat16)
    low = (table - high.astype(np.float32)).astype(ml_dtypes.bfloat16)
    return high, low


def decay(alpha):
    return (-1.0 + np.sqrt(1.0 - 4.0 * alpha * alpha)) / (2.0 * alpha)


def azimuth_tables(cells, blocks):
    total = cells * blocks
    wave = 2.0 * np.pi * np.arange(total) / total
    slope_symbol = 1j * (COEF_A * np.sin(wave) + 0.5 * COEF_B * np.sin(2.0 * wave))
    slope_symbol = slope_symbol / (1.0 + 2.0 * ALPHA_D * np.cos(wave))
    weights = filter_weights()
    smooth_symbol = sum(w * np.cos(n * wave) for n, w in enumerate(weights))
    smooth_symbol = smooth_symbol / (1.0 + 2.0 * ALPHA_F * np.cos(wave))
    slope = np.real(np.fft.ifft(slope_symbol))
    smooth = np.real(np.fft.ifft(smooth_symbol))
    i = np.arange(cells)
    gap = (i[:, None] - i[None, :]) % total
    main = np.concatenate([slope[gap], smooth[gap]], axis=0)
    rate_d, rate_f = decay(ALPHA_D), decay(ALPHA_F)
    scale_d = slope[2] / rate_d**2
    scale_f = smooth[5] / rate_f**5
    send_right = np.stack([rate_d ** (cells - 1 - i), rate_f ** (cells - 1 - i)])
    sums = np.zeros((2 * cells, SUMS))
    sums[:cells, 0] = scale_d * rate_d ** (i + 1)
    sums[cells:, 1] = scale_f * rate_f ** (i + 1)
    raw = np.zeros((2 * cells, RAW))
    for m in range(RAW):
        for row in range(RAW - m):
            n = row + 1 + m
            if n < 2:
                raw[row, RAW - 1 - m] = slope[n] - scale_d * rate_d**n
            if n < 5:
                raw[cells + row, RAW - 1 - m] = smooth[n] - scale_f * rate_f**n
    send_left = send_right[:, ::-1]

    def mirrored(table):
        return np.concatenate([-table[:cells][::-1], table[cells:][::-1]], axis=0)

    uses = np.concatenate([raw, mirrored(raw)[:, ::-1], sums, mirrored(sums)], axis=1)
    return main, np.concatenate([send_right, send_left], axis=0), uses


def radial_matrix(total):
    system = np.eye(total) + ALPHA_D * (np.eye(total, k=1) + np.eye(total, k=-1))
    side = 0.5 * COEF_A * (np.eye(total, k=1) - np.eye(total, k=-1))
    side = side + 0.25 * COEF_B * (np.eye(total, k=2) - np.eye(total, k=-2))
    return np.linalg.solve(system, side)


def rank_two(corner):
    cells = corner.shape[0]
    send = np.zeros((2, cells))
    send[0] = corner[1] / corner[1, cells - 1]
    send[1, cells - 1] = 1.0
    use = np.zeros((cells, 2))
    use[1:, 0] = corner[1:, cells - 1]
    use[0, 0] = corner[0, cells - 2] / send[0, cells - 2]
    use[0, 1] = corner[0, cells - 1] - use[0, 0]
    return use, send


def radial_tables(cells, blocks):
    full = radial_matrix(cells * blocks).reshape(blocks, cells, blocks, cells)
    main = np.stack([full[b, :, b, :] for b in range(blocks)])
    use_left = np.zeros((blocks, cells, 2))
    use_right = np.zeros((blocks, cells, 2))
    send_right = np.zeros((blocks, 2, cells))
    send_left = np.zeros((blocks, 2, cells))
    for b in range(1, blocks):
        use_left[b], send_right[b - 1] = rank_two(full[b, :, b - 1, :])
    for b in range(blocks - 1):
        use, send = rank_two(full[b, :, b + 1, :][::-1, ::-1])
        use_right[b], send_left[b + 1] = use[::-1], send[:, ::-1]
    return main, send_right, send_left, use_left, use_right


def build_tables(cells_t, azi_count, cells_r, rad_count):
    main, edge_sums, edge_uses = azimuth_tables(cells_t, azi_count)
    sends = np.zeros((16, cells_t))
    sends[: 2 * SUMS] = edge_sums
    high, low = split(sends)
    azi_send = np.concatenate([high, low, high], axis=1)
    uses = np.zeros((2 * cells_t, 16))
    uses[:, : edge_uses.shape[1]] = edge_uses
    high, low = split(main)
    use_high, use_low = split(uses)
    azi_main = np.concatenate([high, low, high], axis=1)
    azi_use = np.concatenate([use_high, use_low, use_high], axis=1)

    main, send_right, send_left, use_left, use_right = radial_tables(cells_r, rad_count)
    sends = np.concatenate([send_right, send_left], axis=1)
    high, low = split(sends)
    rad_send = np.zeros((rad_count, 16, 2 * cells_r), ml_dtypes.bfloat16)
    rad_send[:, 0:4, :cells_r] = high
    rad_send[:, 0:4, cells_r:] = high
    rad_send[:, 8:12, :cells_r] = low
    turned = np.swapaxes(main, 1, 2)
    high, low = split(turned)
    rad_main = np.zeros((rad_count, 2 * cells_r, 2 * cells_r), ml_dtypes.bfloat16)
    rad_main[:, :cells_r, :cells_r] = high
    rad_main[:, :cells_r, cells_r:] = low
    rad_main[:, cells_r:, :cells_r] = high
    uses = np.swapaxes(np.concatenate([use_left, use_right], axis=2), 1, 2)
    high, low = split(uses)
    rad_use = np.zeros((rad_count, 16, cells_r), ml_dtypes.bfloat16)
    rad_use[:, 0:4], rad_use[:, 4:8], rad_use[:, 8:12] = high, low, high
    return azi_send, azi_main, azi_use, rad_send, rad_main, rad_use


def halves(x):
    high = x.astype(BF16)
    return high, (x - high.astype(F32)).astype(BF16)


def dot(a, b):
    return jnp.dot(a, b, preferred_element_type=F32)


def block_kernel(
    azi_count, rad_count, chunk,
    fields, azi_send, azi_main, rad_send, rad_main, rad_use, radial_metric,
    raw_left, raw_right, sum_left, sum_right, part_slope, part_smooth, grad_radial,
    block, azi_send_v, azi_main_v, rad_send_v, rad_main_v, rad_use_v, metric,
    to_right, to_left, to_out, to_in, from_in, from_out, ends,
    table_sem, load_sem, send_sem, recv_sem, rad_send_sem, rad_recv_sem, ready,
):
    planes, cells_t, cells_r = block.shape
    count = planes // chunk
    rows = chunk * cells_t
    groups = chunk // PACK
    rad, azi = lax.axis_index("rad"), lax.axis_index("azi")
    right = (rad, lax.rem(azi + 1, azi_count))
    left = (rad, lax.rem(azi + azi_count - 1, azi_count))
    outer = (lax.rem(rad + 1, rad_count), azi)
    inner = (lax.rem(rad + rad_count - 1, rad_count), azi)
    has_outer, has_inner = rad < rad_count - 1, rad > 0
    barrier = pltpu.get_barrier_semaphore()
    pl.semaphore_signal(barrier, inc=1, device_id=left, device_id_type=MESH)

    @pl.when(has_outer)
    def _():
        pl.semaphore_signal(barrier, inc=1, device_id=outer, device_id_type=MESH)

    def load(c):
        span = pl.ds(c * chunk, chunk)
        return pltpu.make_async_copy(fields.at[span], block.at[span], load_sem.at[c])

    tables = [
        pltpu.make_async_copy(source, target, table_sem.at[k])
        for k, (source, target) in enumerate(
            (
                (azi_send, azi_send_v),
                (rad_send.at[rad], rad_send_v),
                (azi_main, azi_main_v),
                (rad_main.at[rad], rad_main_v),
                (rad_use.at[rad], rad_use_v),
                (radial_metric, metric),
            )
        )
    ]

    def send(k, source, target, place):
        return pltpu.make_async_remote_copy(
            src_ref=source,
            dst_ref=target,
            send_sem=send_sem.at[k],
            recv_sem=recv_sem.at[k],
            device_id=place,
            device_id_type=MESH,
        )

    raw_sends = (
        send(0, fields.at[:, pl.ds(cells_t - RAW, RAW)], raw_left, right),
        send(1, fields.at[:, pl.ds(0, RAW)], raw_right, left),
    )
    sum_sends = (send(2, to_right, sum_left, right), send(3, to_left, sum_right, left))
    out_send, in_send = [
        pltpu.make_async_remote_copy(
            src_ref=source,
            dst_ref=target,
            send_sem=rad_send_sem.at[k],
            recv_sem=rad_recv_sem.at[k],
            device_id=place,
            device_id_type=MESH,
        )
        for k, (source, target, place) in enumerate(
            ((to_out, from_in, outer), (to_in, from_out, inner))
        )
    ]

    tables[0].start()
    for c in range(count):
        load(c).start()
    for table in tables[1:]:
        table.start()

    pl.semaphore_wait(barrier, 1 + has_inner.astype(jnp.int32))
    raw_sends[0].start()
    pl.semaphore_signal(ready.at[0], inc=1, device_id=right, device_id_type=MESH)

    @pl.when(has_inner)
    def _():
        pl.semaphore_signal(ready.at[1], inc=1, device_id=inner, device_id_type=MESH)

    tables[0].wait()

    @pl.loop(0, count)
    def _(c):
        load(c).wait()
        high, low = halves(block[pl.ds(c * chunk, chunk)])
        for p in range(0, chunk, 2):
            edge = dot(azi_send_v[...], stacked(high, low, p))
            for k in range(2):
                group, slot = divmod(p + k, PACK)
                lanes = slice(k * cells_r, (k + 1) * cells_r)
                span = slice(SUMS * slot, SUMS * (slot + 1))
                to_right[c * groups + group, span, :] = edge[0:SUMS, lanes]
                to_left[c * groups + group, span, :] = edge[SUMS : 2 * SUMS, lanes]

    sum_sends[0].start()
    tables[1].wait()

    @pl.loop(0, count)
    def _(c):
        high, low = halves(block[pl.ds(c * chunk, chunk)])
        tips = lax.dot_general(
            rad_send_v[...], paired(high, low), (((1,), (1,)), ((), ())),
            preferred_element_type=F32,
        )
        tips = tips[0:8] + tips[8:16]
        span = pl.ds(pl.multiple_of(c * rows, rows), rows)
        to_out[:, span] = tips[0:2]
        to_in[:, span] = tips[2:4]

    @pl.when(has_inner)
    def _():
        in_send.start()

    @pl.when(has_outer)
    def _():
        pl.semaphore_wait(ready.at[1], 1)
        out_send.start()

    pl.semaphore_wait(ready.at[0], 1)
    raw_sends[1].start()
    sum_sends[1].start()
    for table in tables[2:]:
        table.wait()
    ends[...] = jnp.zeros_like(ends)

    @pl.loop(0, count)
    def _(c):
        high, low = halves(block[pl.ds(c * chunk, chunk)])
        for p in range(0, chunk, 2):
            result = dot(azi_main_v[...], stacked(high, low, p))
            for k in range(2):
                lanes = slice(k * cells_r, (k + 1) * cells_r)
                part_slope[c * chunk + p + k] = result[:cells_t, lanes]
                part_smooth[c * chunk + p + k] = result[cells_t:, lanes]

    @pl.when(has_inner)
    def _():
        in_send.wait_send()
        out_send.wait_recv()

    @pl.when(jnp.logical_not(has_inner))
    def _():
        from_in[...] = jnp.zeros_like(from_in)

    @pl.when(has_outer)
    def _():
        out_send.wait_send()
        in_send.wait_recv()

    @pl.when(jnp.logical_not(has_outer))
    def _():
        from_out[...] = jnp.zeros_like(from_out)

    @pl.loop(0, count)
    def _(c):
        span = pl.ds(pl.multiple_of(c * rows, rows), rows)
        ends[0:2] = from_in[:, span]
        ends[2:4] = from_out[:, span]
        rim = ends[0:4]
        rim_high = rim.astype(BF16).astype(F32)
        ends[0:4] = rim_high
        ends[4:8] = rim_high
        ends[8:12] = rim - rim_high
        high, low = halves(block[pl.ds(c * chunk, chunk)])
        both = dot(paired(high, low), rad_main_v[...])
        outside = lax.dot_general(
            ends[...].astype(BF16), rad_use_v[...], (((0,), (0,)), ((), ())),
            preferred_element_type=F32,
        )
        slope = (both[:, :cells_r] + both[:, cells_r:] + outside) * metric[...]
        grad_radial[pl.ds(c * chunk, chunk)] = slope.reshape(chunk, cells_t, cells_r)

    for copy in raw_sends + sum_sends:
        copy.wait()


def stacked(high, low, p):
    return jnp.concatenate(
        [jnp.concatenate([high[q], high[q], low[q]], axis=0) for q in (p, p + 1)], axis=1
    )


def paired(high, low):
    planes, cells_t, cells_r = high.shape
    rows = planes * cells_t
    return jnp.concatenate([high.reshape(rows, cells_r), low.reshape(rows, cells_r)], axis=1)


def join_kernel(
    chunk, part_slope, part_smooth, radial, raw_left, raw_right, sum_left, sum_right,
    azi_use, azimuth_metric,
    grad_azimuth, filtered, grad_radial,
    slopes, smooths, rims, radial_sem, sems,
):
    planes, cells_t, cells_r = part_slope.shape
    count = planes // chunk
    groups = chunk // PACK
    radial_copy = pltpu.make_async_copy(radial, grad_radial, radial_sem)
    radial_copy.start()
    rims[...] = jnp.zeros_like(rims)

    def stores(c):
        span = pl.ds(c * chunk, chunk)
        return [
            pltpu.make_async_copy(source.at[span], target.at[span], sems.at[k, c])
            for k, (source, target) in enumerate(((slopes, grad_azimuth), (smooths, filtered)))
        ]

    @pl.loop(0, count)
    def _(c):
        for p in range(chunk):
            group, slot = divmod(p, PACK)
            span = slice(SUMS * slot, SUMS * (slot + 1))
            rims[p, 0:RAW, :] = raw_left[c * chunk + p]
            rims[p, RAW : 2 * RAW, :] = raw_right[c * chunk + p]
            rims[p, 8:10, :] = sum_left[c * groups + group, span, :]
            rims[p, 10:12, :] = sum_right[c * groups + group, span, :]
        high, low = halves(rims[...])
        for p in range(0, chunk, 2):
            result = dot(azi_use[...], stacked(high, low, p))
            for k in range(2):
                q = c * chunk + p + k
                lanes = slice(k * cells_r, (k + 1) * cells_r)
                slopes[q] = (part_slope[q] + result[:cells_t, lanes]) * azimuth_metric[...]
                smooths[q] = part_smooth[q] + result[cells_t:, lanes]
        for copy in stores(c):
            copy.start()

    @pl.loop(0, count)
    def _(c):
        for copy in stores(c):
            copy.wait()

    radial_copy.wait()


def local(tables, azi_count, rad_count, fields, radial_metric, azimuth_metric):
    azi_send, azi_main, azi_use, rad_send, rad_main, rad_use = [jnp.asarray(t) for t in tables]
    shape = fields.shape
    cells_t, cells_r = shape[2], shape[3]
    planes = shape[0] * shape[1]
    x = fields.reshape(planes, cells_t, cells_r)
    chunk = 8
    count = planes // chunk
    raws = jax.ShapeDtypeStruct((planes, RAW, cells_r), F32)
    sums = jax.ShapeDtypeStruct((planes // PACK, PACK * SUMS, cells_r), F32)
    full = jax.ShapeDtypeStruct(x.shape, F32)
    ends = pltpu.VMEM((2, planes * cells_t), F32)
    hbm = pl.BlockSpec(memory_space=pltpu.HBM)
    vmem = pl.BlockSpec(memory_space=pltpu.VMEM)
    dma = pltpu.SemaphoreType.DMA
    raw_left, raw_right, sum_left, sum_right, part_slope, part_smooth, radial = pl.pallas_call(
        functools.partial(block_kernel, azi_count, rad_count, chunk),
        out_shape=[raws, raws, sums, sums, full, full, full],
        in_specs=[hbm] * 7,
        out_specs=[vmem] * 7,
        scratch_shapes=[
            pltpu.VMEM(x.shape, F32),
            pltpu.VMEM(azi_send.shape, BF16),
            pltpu.VMEM(azi_main.shape, BF16),
            pltpu.VMEM(rad_send.shape[1:], BF16),
            pltpu.VMEM(rad_main.shape[1:], BF16),
            pltpu.VMEM(rad_use.shape[1:], BF16),
            pltpu.VMEM((1, cells_r), F32),
            pltpu.VMEM(sums.shape, F32),
            pltpu.VMEM(sums.shape, F32),
            ends,
            ends,
            ends,
            ends,
            pltpu.VMEM((16, chunk * cells_t), F32),
            dma((6,)),
            dma((count,)),
            dma((4,)),
            dma((4,)),
            dma((2,)),
            dma((2,)),
            pltpu.SemaphoreType.REGULAR((2,)),
        ],
        compiler_params=pltpu.CompilerParams(
            collective_id=0, has_side_effects=True, vmem_limit_bytes=24 * 2**20
        ),
    )(
        *[
            pltpu.with_memory_space_constraint(a, pltpu.HBM)
            for a in (x, azi_send, azi_main, rad_send, rad_main, rad_use, radial_metric.reshape(1, cells_r))
        ]
    )

    outs = pl.pallas_call(
        functools.partial(join_kernel, chunk),
        out_shape=[full] * 3,
        in_specs=[vmem] * 9,
        out_specs=[hbm] * 3,
        scratch_shapes=[
            pltpu.VMEM(x.shape, F32),
            pltpu.VMEM(x.shape, F32),
            pltpu.VMEM((chunk, 16, cells_r), F32),
            dma,
            dma((2, count)),
        ],
        compiler_params=pltpu.CompilerParams(vmem_limit_bytes=24 * 2**20),
    )(
        part_slope, part_smooth, radial, raw_left, raw_right, sum_left, sum_right, azi_use,
        azimuth_metric.reshape(1, cells_r),
    )
    grad_azimuth, filtered, grad_radial = [a.reshape(shape) for a in outs]
    return grad_azimuth, grad_radial, filtered


def solution(mesh):
    rad_count, azi_count = mesh.shape["rad"], mesh.shape["azi"]
    spec = P(None, None, "azi", "rad")

    def run(fields, radial_metric, azimuth_metric):
        tables = build_tables(
            fields.shape[2] // azi_count, azi_count, fields.shape[3] // rad_count, rad_count
        )
        body = functools.partial(local, tables, azi_count, rad_count)
        return jax.shard_map(
            body,
            mesh=mesh,
            in_specs=(spec, P("rad"), P("rad")),
            out_specs=(spec, spec, spec),
            check_vma=False,
        )(fields, radial_metric, azimuth_metric)

    return run
```

```python
import functools

import jax
import jax.numpy as jnp
import ml_dtypes
import numpy as np
from jax import lax
from jax.experimental import pallas as pl
from jax.experimental.pallas import tpu as pltpu
from jax.sharding import PartitionSpec as P

ALPHA_D = 1.0 / 3.0
COEF_A = 14.0 / 9.0
COEF_B = 1.0 / 9.0
ALPHA_F = 0.49
MESH = pl.DeviceIdType.MESH
BF16 = jnp.bfloat16
F32 = jnp.float32

RAW = 4
SUMS = 2
PACK = 4


def filter_weights():
    slack = 1.0 - 2.0 * ALPHA_F
    return [
        (193.0 + 126.0 * ALPHA_F) / 256.0,
        (105.0 + 302.0 * ALPHA_F) / 256.0,
        -15.0 * slack / 64.0,
        45.0 * slack / 512.0,
        -5.0 * slack / 256.0,
        slack / 512.0,
    ]


def split(table):
    table = np.asarray(table, np.float32)
    high = table.astype(ml_dtypes.bfloat16)
    low = (table - high.astype(np.float32)).astype(ml_dtypes.bfloat16)
    return high, low


def decay(alpha):
    return (-1.0 + np.sqrt(1.0 - 4.0 * alpha * alpha)) / (2.0 * alpha)


def azimuth_tables(cells, blocks):
    total = cells * blocks
    wave = 2.0 * np.pi * np.arange(total) / total
    slope_symbol = 1j * (COEF_A * np.sin(wave) + 0.5 * COEF_B * np.sin(2.0 * wave))
    slope_symbol = slope_symbol / (1.0 + 2.0 * ALPHA_D * np.cos(wave))
    weights = filter_weights()
    smooth_symbol = sum(w * np.cos(n * wave) for n, w in enumerate(weights))
    smooth_symbol = smooth_symbol / (1.0 + 2.0 * ALPHA_F * np.cos(wave))
    slope = np.real(np.fft.ifft(slope_symbol))
    smooth = np.real(np.fft.ifft(smooth_symbol))
    i = np.arange(cells)
    gap = (i[:, None] - i[None, :]) % total
    main = np.concatenate([slope[gap], smooth[gap]], axis=0)
    rate_d, rate_f = decay(ALPHA_D), decay(ALPHA_F)
    scale_d = slope[2] / rate_d**2
    scale_f = smooth[5] / rate_f**5
    send_right = np.stack([rate_d ** (cells - 1 - i), rate_f ** (cells - 1 - i)])
    sums = np.zeros((2 * cells, SUMS))
    sums[:cells, 0] = scale_d * rate_d ** (i + 1)
    sums[cells:, 1] = scale_f * rate_f ** (i + 1)
    raw = np.zeros((2 * cells, RAW))
    for m in range(RAW):
        for row in range(RAW - m):
            n = row + 1 + m
            if n < 2:
                raw[row, RAW - 1 - m] = slope[n] - scale_d * rate_d**n
            if n < 5:
                raw[cells + row, RAW - 1 - m] = smooth[n] - scale_f * rate_f**n
    send_left = send_right[:, ::-1]

    def mirrored(table):
        return np.concatenate([-table[:cells][::-1], table[cells:][::-1]], axis=0)

    uses = np.concatenate([raw, mirrored(raw)[:, ::-1], sums, mirrored(sums)], axis=1)
    return main, np.concatenate([send_right, send_left], axis=0), uses


def radial_matrix(total):
    system = np.eye(total) + ALPHA_D * (np.eye(total, k=1) + np.eye(total, k=-1))
    side = 0.5 * COEF_A * (np.eye(total, k=1) - np.eye(total, k=-1))
    side = side + 0.25 * COEF_B * (np.eye(total, k=2) - np.eye(total, k=-2))
    return np.linalg.solve(system, side)


def rank_two(corner):
    cells = corner.shape[0]
    send = np.zeros((2, cells))
    send[0] = corner[1] / corner[1, cells - 1]
    send[1, cells - 1] = 1.0
    use = np.zeros((cells, 2))
    use[1:, 0] = corner[1:, cells - 1]
    use[0, 0] = corner[0, cells - 2] / send[0, cells - 2]
    use[0, 1] = corner[0, cells - 1] - use[0, 0]
    return use, send


def radial_tables(cells, blocks):
    full = radial_matrix(cells * blocks).reshape(blocks, cells, blocks, cells)
    main = np.stack([full[b, :, b, :] for b in range(blocks)])
    use_left = np.zeros((blocks, cells, 2))
    use_right = np.zeros((blocks, cells, 2))
    send_right = np.zeros((blocks, 2, cells))
    send_left = np.zeros((blocks, 2, cells))
    for b in range(1, blocks):
        use_left[b], send_right[b - 1] = rank_two(full[b, :, b - 1, :])
    for b in range(blocks - 1):
        use, send = rank_two(full[b, :, b + 1, :][::-1, ::-1])
        use_right[b], send_left[b + 1] = use[::-1], send[:, ::-1]
    return main, send_right, send_left, use_left, use_right


def build_tables(cells_t, azi_count, cells_r, rad_count):
    main, edge_sums, edge_uses = azimuth_tables(cells_t, azi_count)
    sends = np.zeros((16, cells_t))
    sends[: 2 * SUMS] = edge_sums
    high, low = split(sends)
    azi_send = np.concatenate([high, low, high], axis=1)
    uses = np.zeros((2 * cells_t, 16))
    uses[:, : edge_uses.shape[1]] = edge_uses
    high, low = split(main)
    use_high, use_low = split(uses)
    azi_main = np.concatenate([high, low, high], axis=1)
    azi_use = np.concatenate([use_high, use_low, use_high], axis=1)

    main, send_right, send_left, use_left, use_right = radial_tables(cells_r, rad_count)
    sends = np.concatenate([send_right, send_left], axis=1)
    high, low = split(sends)
    rad_send = np.zeros((rad_count, 16, 2 * cells_r), ml_dtypes.bfloat16)
    rad_send[:, 0:4, :cells_r] = high
    rad_send[:, 0:4, cells_r:] = high
    rad_send[:, 8:12, :cells_r] = low
    turned = np.swapaxes(main, 1, 2)
    high, low = split(turned)
    rad_main = np.zeros((rad_count, 2 * cells_r, 2 * cells_r), ml_dtypes.bfloat16)
    rad_main[:, :cells_r, :cells_r] = high
    rad_main[:, :cells_r, cells_r:] = low
    rad_main[:, cells_r:, :cells_r] = high
    uses = np.swapaxes(np.concatenate([use_left, use_right], axis=2), 1, 2)
    high, low = split(uses)
    rad_use = np.zeros((rad_count, 16, cells_r), ml_dtypes.bfloat16)
    rad_use[:, 0:4], rad_use[:, 4:8], rad_use[:, 8:12] = high, low, high
    return azi_send, azi_main, azi_use, rad_send, rad_main, rad_use


def halves(x):
    high = x.astype(BF16)
    return high, (x - high.astype(F32)).astype(BF16)


def dot(a, b):
    return jnp.dot(a, b, preferred_element_type=F32)


def block_kernel(
    azi_count, rad_count, chunk,
    fields, azi_send, azi_main, rad_send, rad_main, rad_use, radial_metric,
    raw_left, raw_right, sum_left, sum_right, part_slope, part_smooth, grad_radial,
    block, azi_send_v, azi_main_v, rad_send_v, rad_main_v, rad_use_v, metric,
    to_right, to_left, to_out, to_in, from_in, from_out, ends,
    table_sem, load_sem, send_sem, recv_sem, rad_send_sem, rad_recv_sem, ready,
):
    planes, cells_t, cells_r = block.shape
    count = planes // chunk
    rows = chunk * cells_t
    groups = chunk // PACK
    rad, azi = lax.axis_index("rad"), lax.axis_index("azi")
    right = (rad, lax.rem(azi + 1, azi_count))
    left = (rad, lax.rem(azi + azi_count - 1, azi_count))
    outer = (lax.rem(rad + 1, rad_count), azi)
    inner = (lax.rem(rad + rad_count - 1, rad_count), azi)
    has_outer, has_inner = rad < rad_count - 1, rad > 0
    is_first, is_last = azi == 0, azi == azi_count - 1
    is_second, is_third = azi == 1, azi == 2
    early = jnp.logical_or(is_second, is_last)
    even = lax.rem(rad, 2) == 0
    odd = jnp.logical_not(even)
    barrier = pltpu.get_barrier_semaphore()

    @pl.when(jnp.logical_not(is_third))
    def _():
        pl.semaphore_signal(barrier, inc=1, device_id=left, device_id_type=MESH)

    @pl.when(jnp.logical_not(is_last))
    def _():
        pl.semaphore_signal(barrier, inc=1, device_id=right, device_id_type=MESH)

    @pl.when(jnp.logical_and(odd, has_outer))
    def _():
        pl.semaphore_signal(barrier, inc=1, device_id=outer, device_id_type=MESH)

    @pl.when(odd)
    def _():
        pl.semaphore_signal(barrier, inc=1, device_id=inner, device_id_type=MESH)

    def load(c):
        span = pl.ds(c * chunk, chunk)
        return pltpu.make_async_copy(fields.at[span], block.at[span], load_sem.at[c])

    tables = [
        pltpu.make_async_copy(source, target, table_sem.at[k])
        for k, (source, target) in enumerate(
            (
                (azi_send, azi_send_v),
                (rad_send.at[rad], rad_send_v),
                (azi_main, azi_main_v),
                (rad_main.at[rad], rad_main_v),
                (rad_use.at[rad], rad_use_v),
                (radial_metric, metric),
            )
        )
    ]

    def send(k, source, target, place):
        return pltpu.make_async_remote_copy(
            src_ref=source,
            dst_ref=target,
            send_sem=send_sem.at[k],
            recv_sem=recv_sem.at[k],
            device_id=place,
            device_id_type=MESH,
        )

    raw_sends = (
        send(0, fields.at[:, pl.ds(cells_t - RAW, RAW)], raw_left, right),
        send(1, fields.at[:, pl.ds(0, RAW)], raw_right, left),
    )
    sum_sends = (send(2, to_right, sum_left, right), send(3, to_left, sum_right, left))
    out_send, in_send = [
        pltpu.make_async_remote_copy(
            src_ref=source,
            dst_ref=target,
            send_sem=rad_send_sem.at[k],
            recv_sem=rad_recv_sem.at[k],
            device_id=place,
            device_id_type=MESH,
        )
        for k, (source, target, place) in enumerate(
            ((to_out, from_in, outer), (to_in, from_out, inner))
        )
    ]

    tables[0].start()
    for c in range(count):
        load(c).start()
    for table in tables[1:]:
        table.start()

    def first(pair):
        @pl.when(right_first)
        def _():
            pair[0].start()

        @pl.when(jnp.logical_not(right_first))
        def _():
            pair[1].start()

    def second(pair):
        @pl.when(right_first)
        def _():
            pair[1].start()

        @pl.when(jnp.logical_not(right_first))
        def _():
            pair[0].start()

    def greet():
        neighbours = jnp.where(azi < 2, 1, 2)
        beside = has_inner.astype(jnp.int32) + has_outer.astype(jnp.int32)
        pl.semaphore_wait(barrier, neighbours + jnp.where(even, beside, 0))

        @pl.when(is_last)
        def _():
            pl.semaphore_signal(ready.at[0], inc=1, device_id=right, device_id_type=MESH)

        @pl.when(is_third)
        def _():
            pl.semaphore_signal(ready.at[0], inc=1, device_id=left, device_id_type=MESH)

        @pl.when(jnp.logical_and(even, has_inner))
        def _():
            pl.semaphore_signal(ready.at[1], inc=1, device_id=inner, device_id_type=MESH)

        @pl.when(jnp.logical_and(even, has_outer))
        def _():
            pl.semaphore_signal(ready.at[2], inc=1, device_id=outer, device_id_type=MESH)

    @pl.when(early)
    def _():
        greet()

        @pl.when(is_last)
        def _():
            raw_sends[0].start()

        raw_sends[1].start()

    tables[0].wait()

    @pl.loop(0, count)
    def _(c):
        load(c).wait()
        high, low = halves(block[pl.ds(c * chunk, chunk)])
        for p in range(0, chunk, 2):
            edge = dot(azi_send_v[...], stacked(high, low, p))
            for k in range(2):
                group, slot = divmod(p + k, PACK)
                lanes = slice(k * cells_r, (k + 1) * cells_r)
                span = slice(SUMS * slot, SUMS * (slot + 1))
                to_right[c * groups + group, span, :] = edge[0:SUMS, lanes]
                to_left[c * groups + group, span, :] = edge[SUMS : 2 * SUMS, lanes]

    @pl.when(early)
    def _():
        @pl.when(is_last)
        def _():
            sum_sends[0].start()

        sum_sends[1].start()

    @pl.when(jnp.logical_not(early))
    def _():
        greet()

        @pl.when(jnp.logical_not(is_first))
        def _():
            raw_sends[1].start()
            sum_sends[1].start()

        raw_sends[0].start()
        sum_sends[0].start()

    tables[1].wait()

    @pl.loop(0, count)
    def _(c):
        high, low = halves(block[pl.ds(c * chunk, chunk)])
        tips = lax.dot_general(
            rad_send_v[...], paired(high, low), (((1,), (1,)), ((), ())),
            preferred_element_type=F32,
        )
        tips = tips[0:8] + tips[8:16]
        span = pl.ds(pl.multiple_of(c * rows, rows), rows)
        to_out[:, span] = tips[0:2]
        to_in[:, span] = tips[2:4]

    @pl.when(has_inner)
    def _():
        @pl.when(odd)
        def _():
            pl.semaphore_wait(ready.at[2], 1)

        in_send.start()

    @pl.when(has_outer)
    def _():
        @pl.when(odd)
        def _():
            pl.semaphore_wait(ready.at[1], 1)

        out_send.start()

    @pl.when(is_second)
    def _():
        pl.semaphore_wait(ready.at[0], 1)
        raw_sends[0].start()
        sum_sends[0].start()

    for table in tables[2:]:
        table.wait()
    ends[...] = jnp.zeros_like(ends)

    @pl.loop(0, count)
    def _(c):
        high, low = halves(block[pl.ds(c * chunk, chunk)])
        for p in range(0, chunk, 2):
            result = dot(azi_main_v[...], stacked(high, low, p))
            for k in range(2):
                lanes = slice(k * cells_r, (k + 1) * cells_r)
                part_slope[c * chunk + p + k] = result[:cells_t, lanes]
                part_smooth[c * chunk + p + k] = result[cells_t:, lanes]

    @pl.when(is_first)
    def _():
        pl.semaphore_wait(ready.at[0], 1)
        raw_sends[1].start()
        sum_sends[1].start()

    @pl.when(has_inner)
    def _():
        in_send.wait_send()
        out_send.wait_recv()

    @pl.when(jnp.logical_not(has_inner))
    def _():
        from_in[...] = jnp.zeros_like(from_in)

    @pl.when(has_outer)
    def _():
        out_send.wait_send()
        in_send.wait_recv()

    @pl.when(jnp.logical_not(has_outer))
    def _():
        from_out[...] = jnp.zeros_like(from_out)

    @pl.loop(0, count)
    def _(c):
        span = pl.ds(pl.multiple_of(c * rows, rows), rows)
        ends[0:2] = from_in[:, span]
        ends[2:4] = from_out[:, span]
        rim = ends[0:4]
        rim_high = rim.astype(BF16).astype(F32)
        ends[0:4] = rim_high
        ends[4:8] = rim_high
        ends[8:12] = rim - rim_high
        high, low = halves(block[pl.ds(c * chunk, chunk)])
        both = dot(paired(high, low), rad_main_v[...])
        outside = lax.dot_general(
            ends[...].astype(BF16), rad_use_v[...], (((0,), (0,)), ((), ())),
            preferred_element_type=F32,
        )
        slope = (both[:, :cells_r] + both[:, cells_r:] + outside) * metric[...]
        grad_radial[pl.ds(c * chunk, chunk)] = slope.reshape(chunk, cells_t, cells_r)

    for copy in raw_sends + sum_sends:
        copy.wait()


def stacked(high, low, p):
    return jnp.concatenate(
        [jnp.concatenate([high[q], high[q], low[q]], axis=0) for q in (p, p + 1)], axis=1
    )


def paired(high, low):
    planes, cells_t, cells_r = high.shape
    rows = planes * cells_t
    return jnp.concatenate([high.reshape(rows, cells_r), low.reshape(rows, cells_r)], axis=1)


def join_kernel(
    chunk, part_slope, part_smooth, radial, raw_left, raw_right, sum_left, sum_right,
    azi_use, azimuth_metric,
    grad_azimuth, filtered, grad_radial,
    slopes, smooths, rims, radial_sem, sems,
):
    planes, cells_t, cells_r = part_slope.shape
    count = planes // chunk
    groups = chunk // PACK
    radial_copy = pltpu.make_async_copy(radial, grad_radial, radial_sem)
    radial_copy.start()
    rims[...] = jnp.zeros_like(rims)

    def stores(c):
        span = pl.ds(c * chunk, chunk)
        return [
            pltpu.make_async_copy(source.at[span], target.at[span], sems.at[k, c])
            for k, (source, target) in enumerate(((slopes, grad_azimuth), (smooths, filtered)))
        ]

    @pl.loop(0, count)
    def _(c):
        for p in range(chunk):
            group, slot = divmod(p, PACK)
            span = slice(SUMS * slot, SUMS * (slot + 1))
            rims[p, 0:RAW, :] = raw_left[c * chunk + p]
            rims[p, RAW : 2 * RAW, :] = raw_right[c * chunk + p]
            rims[p, 8:10, :] = sum_left[c * groups + group, span, :]
            rims[p, 10:12, :] = sum_right[c * groups + group, span, :]
        high, low = halves(rims[...])
        for p in range(0, chunk, 2):
            result = dot(azi_use[...], stacked(high, low, p))
            for k in range(2):
                q = c * chunk + p + k
                lanes = slice(k * cells_r, (k + 1) * cells_r)
                slopes[q] = (part_slope[q] + result[:cells_t, lanes]) * azimuth_metric[...]
                smooths[q] = part_smooth[q] + result[cells_t:, lanes]
        for copy in stores(c):
            copy.start()

    @pl.loop(0, count)
    def _(c):
        for copy in stores(c):
            copy.wait()

    radial_copy.wait()


def local(tables, azi_count, rad_count, fields, radial_metric, azimuth_metric):
    azi_send, azi_main, azi_use, rad_send, rad_main, rad_use = [jnp.asarray(t) for t in tables]
    shape = fields.shape
    cells_t, cells_r = shape[2], shape[3]
    planes = shape[0] * shape[1]
    x = fields.reshape(planes, cells_t, cells_r)
    chunk = 8
    count = planes // chunk
    raws = jax.ShapeDtypeStruct((planes, RAW, cells_r), F32)
    sums = jax.ShapeDtypeStruct((planes // PACK, PACK * SUMS, cells_r), F32)
    full = jax.ShapeDtypeStruct(x.shape, F32)
    ends = pltpu.VMEM((2, planes * cells_t), F32)
    hbm = pl.BlockSpec(memory_space=pltpu.HBM)
    vmem = pl.BlockSpec(memory_space=pltpu.VMEM)
    dma = pltpu.SemaphoreType.DMA
    raw_left, raw_right, sum_left, sum_right, part_slope, part_smooth, radial = pl.pallas_call(
        functools.partial(block_kernel, azi_count, rad_count, chunk),
        out_shape=[raws, raws, sums, sums, full, full, full],
        in_specs=[hbm] * 7,
        out_specs=[vmem] * 7,
        scratch_shapes=[
            pltpu.VMEM(x.shape, F32),
            pltpu.VMEM(azi_send.shape, BF16),
            pltpu.VMEM(azi_main.shape, BF16),
            pltpu.VMEM(rad_send.shape[1:], BF16),
            pltpu.VMEM(rad_main.shape[1:], BF16),
            pltpu.VMEM(rad_use.shape[1:], BF16),
            pltpu.VMEM((1, cells_r), F32),
            pltpu.VMEM(sums.shape, F32),
            pltpu.VMEM(sums.shape, F32),
            ends,
            ends,
            ends,
            ends,
            pltpu.VMEM((16, chunk * cells_t), F32),
            dma((6,)),
            dma((count,)),
            dma((4,)),
            dma((4,)),
            dma((2,)),
            dma((2,)),
            pltpu.SemaphoreType.REGULAR((3,)),
        ],
        compiler_params=pltpu.CompilerParams(
            collective_id=0, has_side_effects=True, vmem_limit_bytes=24 * 2**20
        ),
    )(
        *[
            pltpu.with_memory_space_constraint(a, pltpu.HBM)
            for a in (x, azi_send, azi_main, rad_send, rad_main, rad_use, radial_metric.reshape(1, cells_r))
        ]
    )

    outs = pl.pallas_call(
        functools.partial(join_kernel, chunk),
        out_shape=[full] * 3,
        in_specs=[vmem] * 9,
        out_specs=[hbm] * 3,
        scratch_shapes=[
            pltpu.VMEM(x.shape, F32),
            pltpu.VMEM(x.shape, F32),
            pltpu.VMEM((chunk, 16, cells_r), F32),
            dma,
            dma((2, count)),
        ],
        compiler_params=pltpu.CompilerParams(vmem_limit_bytes=24 * 2**20),
    )(
        part_slope, part_smooth, radial, raw_left, raw_right, sum_left, sum_right, azi_use,
        azimuth_metric.reshape(1, cells_r),
    )
    grad_azimuth, filtered, grad_radial = [a.reshape(shape) for a in outs]
    return grad_azimuth, grad_radial, filtered


def solution(mesh):
    rad_count, azi_count = mesh.shape["rad"], mesh.shape["azi"]
    spec = P(None, None, "azi", "rad")

    def run(fields, radial_metric, azimuth_metric):
        tables = build_tables(
            fields.shape[2] // azi_count, azi_count, fields.shape[3] // rad_count, rad_count
        )
        body = functools.partial(local, tables, azi_count, rad_count)
        return jax.shard_map(
            body,
            mesh=mesh,
            in_specs=(spec, P("rad"), P("rad")),
            out_specs=(spec, spec, spec),
            check_vma=False,
        )(fields, radial_metric, azimuth_metric)

    return run
```

```python
import functools

import jax
import jax.numpy as jnp
import ml_dtypes
import numpy as np
from jax import lax
from jax.experimental import pallas as pl
from jax.experimental.pallas import tpu as pltpu
from jax.sharding import PartitionSpec as P

ALPHA_D = 1.0 / 3.0
COEF_A = 14.0 / 9.0
COEF_B = 1.0 / 9.0
ALPHA_F = 0.49
MESH = pl.DeviceIdType.MESH
BF16 = jnp.bfloat16
F32 = jnp.float32

RAW = 4
SUMS = 2
PACK = 4


def filter_weights():
    slack = 1.0 - 2.0 * ALPHA_F
    return [
        (193.0 + 126.0 * ALPHA_F) / 256.0,
        (105.0 + 302.0 * ALPHA_F) / 256.0,
        -15.0 * slack / 64.0,
        45.0 * slack / 512.0,
        -5.0 * slack / 256.0,
        slack / 512.0,
    ]


def split(table):
    table = np.asarray(table, np.float32)
    high = table.astype(ml_dtypes.bfloat16)
    low = (table - high.astype(np.float32)).astype(ml_dtypes.bfloat16)
    return high, low


def decay(alpha):
    return (-1.0 + np.sqrt(1.0 - 4.0 * alpha * alpha)) / (2.0 * alpha)


def azimuth_tables(cells, blocks):
    total = cells * blocks
    wave = 2.0 * np.pi * np.arange(total) / total
    slope_symbol = 1j * (COEF_A * np.sin(wave) + 0.5 * COEF_B * np.sin(2.0 * wave))
    slope_symbol = slope_symbol / (1.0 + 2.0 * ALPHA_D * np.cos(wave))
    weights = filter_weights()
    smooth_symbol = sum(w * np.cos(n * wave) for n, w in enumerate(weights))
    smooth_symbol = smooth_symbol / (1.0 + 2.0 * ALPHA_F * np.cos(wave))
    slope = np.real(np.fft.ifft(slope_symbol))
    smooth = np.real(np.fft.ifft(smooth_symbol))
    i = np.arange(cells)
    gap = (i[:, None] - i[None, :]) % total
    main = np.concatenate([slope[gap], smooth[gap]], axis=0)
    rate_d, rate_f = decay(ALPHA_D), decay(ALPHA_F)
    scale_d = slope[2] / rate_d**2
    scale_f = smooth[5] / rate_f**5
    send_right = np.stack([rate_d ** (cells - 1 - i), rate_f ** (cells - 1 - i)])
    sums = np.zeros((2 * cells, SUMS))
    sums[:cells, 0] = scale_d * rate_d ** (i + 1)
    sums[cells:, 1] = scale_f * rate_f ** (i + 1)
    raw = np.zeros((2 * cells, RAW))
    for m in range(RAW):
        for row in range(RAW - m):
            n = row + 1 + m
            if n < 2:
                raw[row, RAW - 1 - m] = slope[n] - scale_d * rate_d**n
            if n < 5:
                raw[cells + row, RAW - 1 - m] = smooth[n] - scale_f * rate_f**n
    send_left = send_right[:, ::-1]

    def mirrored(table):
        return np.concatenate([-table[:cells][::-1], table[cells:][::-1]], axis=0)

    uses = np.concatenate([raw, mirrored(raw)[:, ::-1], sums, mirrored(sums)], axis=1)
    return main, np.concatenate([send_right, send_left], axis=0), uses


def radial_matrix(total):
    system = np.eye(total) + ALPHA_D * (np.eye(total, k=1) + np.eye(total, k=-1))
    side = 0.5 * COEF_A * (np.eye(total, k=1) - np.eye(total, k=-1))
    side = side + 0.25 * COEF_B * (np.eye(total, k=2) - np.eye(total, k=-2))
    return np.linalg.solve(system, side)


def rank_two(corner):
    cells = corner.shape[0]
    send = np.zeros((2, cells))
    send[0] = corner[1] / corner[1, cells - 1]
    send[1, cells - 1] = 1.0
    use = np.zeros((cells, 2))
    use[1:, 0] = corner[1:, cells - 1]
    use[0, 0] = corner[0, cells - 2] / send[0, cells - 2]
    use[0, 1] = corner[0, cells - 1] - use[0, 0]
    return use, send


def radial_tables(cells, blocks):
    full = radial_matrix(cells * blocks).reshape(blocks, cells, blocks, cells)
    main = np.stack([full[b, :, b, :] for b in range(blocks)])
    use_left = np.zeros((blocks, cells, 2))
    use_right = np.zeros((blocks, cells, 2))
    send_right = np.zeros((blocks, 2, cells))
    send_left = np.zeros((blocks, 2, cells))
    for b in range(1, blocks):
        use_left[b], send_right[b - 1] = rank_two(full[b, :, b - 1, :])
    for b in range(blocks - 1):
        use, send = rank_two(full[b, :, b + 1, :][::-1, ::-1])
        use_right[b], send_left[b + 1] = use[::-1], send[:, ::-1]
    return main, send_right, send_left, use_left, use_right


def build_tables(cells_t, azi_count, cells_r, rad_count):
    main, edge_sums, edge_uses = azimuth_tables(cells_t, azi_count)
    sends = np.zeros((16, cells_t))
    sends[: 2 * SUMS] = edge_sums
    high, low = split(sends)
    azi_send = np.concatenate([high, low, high], axis=1)
    uses = np.zeros((2 * cells_t, 16))
    uses[:, : edge_uses.shape[1]] = edge_uses
    high, low = split(main)
    use_high, use_low = split(uses)
    azi_main = np.concatenate([high, low, high], axis=1)
    azi_use = np.concatenate([use_high, use_low, use_high], axis=1)

    main, send_right, send_left, use_left, use_right = radial_tables(cells_r, rad_count)
    sends = np.concatenate([send_right, send_left], axis=1)
    high, low = split(sends)
    rad_send = np.zeros((rad_count, 16, 2 * cells_r), ml_dtypes.bfloat16)
    rad_send[:, 0:4, :cells_r] = high
    rad_send[:, 0:4, cells_r:] = high
    rad_send[:, 8:12, :cells_r] = low
    turned = np.swapaxes(main, 1, 2)
    high, low = split(turned)
    rad_main = np.zeros((rad_count, 2 * cells_r, 2 * cells_r), ml_dtypes.bfloat16)
    rad_main[:, :cells_r, :cells_r] = high
    rad_main[:, :cells_r, cells_r:] = low
    rad_main[:, cells_r:, :cells_r] = high
    uses = np.swapaxes(np.concatenate([use_left, use_right], axis=2), 1, 2)
    high, low = split(uses)
    rad_use = np.zeros((rad_count, 16, cells_r), ml_dtypes.bfloat16)
    rad_use[:, 0:4], rad_use[:, 4:8], rad_use[:, 8:12] = high, low, high
    return azi_send, azi_main, azi_use, rad_send, rad_main, rad_use


def halves(x):
    high = x.astype(BF16)
    return high, (x - high.astype(F32)).astype(BF16)


def dot(a, b):
    return jnp.dot(a, b, preferred_element_type=F32)


def block_kernel(
    azi_count, rad_count, chunk,
    fields, azi_send, azi_main, rad_send, rad_main, rad_use, radial_metric,
    raw_left, raw_right, sum_left, sum_right, part_slope, part_smooth, grad_radial,
    block, azi_send_v, azi_main_v, rad_send_v, rad_main_v, rad_use_v, metric,
    to_right, to_left, to_out, to_in, from_in, from_out, ends,
    table_sem, load_sem, send_sem, recv_sem, rad_send_sem, rad_recv_sem, ready,
):
    planes, cells_t, cells_r = block.shape
    count = planes // chunk
    rows = chunk * cells_t
    groups = chunk // PACK
    rad, azi = lax.axis_index("rad"), lax.axis_index("azi")
    right = (rad, lax.rem(azi + 1, azi_count))
    left = (rad, lax.rem(azi + azi_count - 1, azi_count))
    outer = (lax.rem(rad + 1, rad_count), azi)
    inner = (lax.rem(rad + rad_count - 1, rad_count), azi)
    has_outer, has_inner = rad < rad_count - 1, rad > 0
    is_first, is_last = azi == 0, azi == azi_count - 1
    last = azi_count - 1
    early = jnp.logical_and(lax.rem(azi, 2) == 1, azi != last - 2)
    tells_left = jnp.logical_and(lax.rem(azi, 2) == 0, jnp.logical_and(azi > 0, azi < last - 1))
    late = jnp.logical_not(early)
    even = lax.rem(rad, 2) == 0
    odd = jnp.logical_not(even)
    barrier = pltpu.get_barrier_semaphore()

    @pl.when(jnp.logical_not(tells_left))
    def _():
        pl.semaphore_signal(barrier, inc=1, device_id=left, device_id_type=MESH)

    @pl.when(azi < azi_count - 2)
    def _():
        pl.semaphore_signal(barrier, inc=1, device_id=right, device_id_type=MESH)

    @pl.when(jnp.logical_and(odd, has_outer))
    def _():
        pl.semaphore_signal(barrier, inc=1, device_id=outer, device_id_type=MESH)

    @pl.when(odd)
    def _():
        pl.semaphore_signal(barrier, inc=1, device_id=inner, device_id_type=MESH)

    def load(c):
        span = pl.ds(c * chunk, chunk)
        return pltpu.make_async_copy(fields.at[span], block.at[span], load_sem.at[c])

    tables = [
        pltpu.make_async_copy(source, target, table_sem.at[k])
        for k, (source, target) in enumerate(
            (
                (azi_send, azi_send_v),
                (rad_send.at[rad], rad_send_v),
                (azi_main, azi_main_v),
                (rad_main.at[rad], rad_main_v),
                (rad_use.at[rad], rad_use_v),
                (radial_metric, metric),
            )
        )
    ]

    def send(k, source, target, place):
        return pltpu.make_async_remote_copy(
            src_ref=source,
            dst_ref=target,
            send_sem=send_sem.at[k],
            recv_sem=recv_sem.at[k],
            device_id=place,
            device_id_type=MESH,
        )

    raw_sends = (
        send(0, fields.at[:, pl.ds(cells_t - RAW, RAW)], raw_left, right),
        send(1, fields.at[:, pl.ds(0, RAW)], raw_right, left),
    )
    cuts = [0, count - 2, count]

    def sums(part):
        span = pl.ds(cuts[part] * groups, (cuts[part + 1] - cuts[part]) * groups)
        return (
            send(2 + 2 * part, to_right.at[span], sum_left.at[span], right),
            send(3 + 2 * part, to_left.at[span], sum_right.at[span], left),
        )

    sum_sends = [sums(part) for part in range(len(cuts) - 1)]
    out_send, in_send = [
        pltpu.make_async_remote_copy(
            src_ref=source,
            dst_ref=target,
            send_sem=rad_send_sem.at[k],
            recv_sem=rad_recv_sem.at[k],
            device_id=place,
            device_id_type=MESH,
        )
        for k, (source, target, place) in enumerate(
            ((to_out, from_in, outer), (to_in, from_out, inner))
        )
    ]

    tables[0].start()
    for c in range(count):
        load(c).start()
    for table in tables[1:]:
        table.start()

    def first(pair):
        @pl.when(right_first)
        def _():
            pair[0].start()

        @pl.when(jnp.logical_not(right_first))
        def _():
            pair[1].start()

    def second(pair):
        @pl.when(right_first)
        def _():
            pair[1].start()

        @pl.when(jnp.logical_not(right_first))
        def _():
            pair[0].start()

    def early_first(pair):
        @pl.when(is_last)
        def _():
            pair[0].start()

        @pl.when(jnp.logical_and(early, jnp.logical_not(is_last)))
        def _():
            pair[1].start()

    def early_second(pair):
        @pl.when(is_last)
        def _():
            pair[1].start()

        @pl.when(jnp.logical_and(early, jnp.logical_not(is_last)))
        def _():
            pair[0].start()

    def greet():
        neighbours = jnp.where(jnp.logical_or(early, is_first), 1, 2)
        beside = has_inner.astype(jnp.int32) + has_outer.astype(jnp.int32)
        pl.semaphore_wait(barrier, neighbours + jnp.where(even, beside, 0))

        @pl.when(azi >= azi_count - 2)
        def _():
            pl.semaphore_signal(ready.at[0], inc=1, device_id=right, device_id_type=MESH)

        @pl.when(tells_left)
        def _():
            pl.semaphore_signal(ready.at[0], inc=1, device_id=left, device_id_type=MESH)

        @pl.when(jnp.logical_and(even, has_inner))
        def _():
            pl.semaphore_signal(ready.at[1], inc=1, device_id=inner, device_id_type=MESH)

        @pl.when(jnp.logical_and(even, has_outer))
        def _():
            pl.semaphore_signal(ready.at[2], inc=1, device_id=outer, device_id_type=MESH)

    @pl.when(early)
    def _():
        greet()

    early_first(raw_sends)
    tables[0].wait()

    def edges(c):
        load(c).wait()
        high, low = halves(block[pl.ds(c * chunk, chunk)])
        for p in range(0, chunk, 2):
            edge = dot(azi_send_v[...], stacked(high, low, p))
            for k in range(2):
                group, slot = divmod(p + k, PACK)
                lanes = slice(k * cells_r, (k + 1) * cells_r)
                span = slice(SUMS * slot, SUMS * (slot + 1))
                to_right[c * groups + group, span, :] = edge[0:SUMS, lanes]
                to_left[c * groups + group, span, :] = edge[SUMS : 2 * SUMS, lanes]

    for part in range(len(cuts) - 1):
        pl.loop(cuts[part], cuts[part + 1])(edges)
        early_first(sum_sends[part])

    @pl.when(late)
    def _():
        greet()

        @pl.when(jnp.logical_not(is_first))
        def _():
            raw_sends[1].start()
            for pair in sum_sends:
                pair[1].start()

        raw_sends[0].start()
        for pair in sum_sends:
            pair[0].start()

    tables[1].wait()

    @pl.loop(0, count)
    def _(c):
        high, low = halves(block[pl.ds(c * chunk, chunk)])
        tips = lax.dot_general(
            rad_send_v[...], paired(high, low), (((1,), (1,)), ((), ())),
            preferred_element_type=F32,
        )
        tips = tips[0:8] + tips[8:16]
        span = pl.ds(pl.multiple_of(c * rows, rows), rows)
        to_out[:, span] = tips[0:2]
        to_in[:, span] = tips[2:4]

    @pl.when(has_inner)
    def _():
        @pl.when(odd)
        def _():
            pl.semaphore_wait(ready.at[2], 1)

        in_send.start()

    @pl.when(has_outer)
    def _():
        @pl.when(odd)
        def _():
            pl.semaphore_wait(ready.at[1], 1)

        out_send.start()

    @pl.when(early)
    def _():
        pl.semaphore_wait(ready.at[0], 1)

    early_second(raw_sends)
    for pair in sum_sends:
        early_second(pair)

    for table in tables[2:]:
        table.wait()
    ends[...] = jnp.zeros_like(ends)

    @pl.loop(0, count)
    def _(c):
        high, low = halves(block[pl.ds(c * chunk, chunk)])
        for p in range(0, chunk, 2):
            result = dot(azi_main_v[...], stacked(high, low, p))
            for k in range(2):
                lanes = slice(k * cells_r, (k + 1) * cells_r)
                part_slope[c * chunk + p + k] = result[:cells_t, lanes]
                part_smooth[c * chunk + p + k] = result[cells_t:, lanes]

    @pl.when(is_first)
    def _():
        pl.semaphore_wait(ready.at[0], 1)
        raw_sends[1].start()
        for pair in sum_sends:
            pair[1].start()

    @pl.when(has_inner)
    def _():
        in_send.wait_send()
        out_send.wait_recv()

    @pl.when(jnp.logical_not(has_inner))
    def _():
        from_in[...] = jnp.zeros_like(from_in)

    @pl.when(has_outer)
    def _():
        out_send.wait_send()
        in_send.wait_recv()

    @pl.when(jnp.logical_not(has_outer))
    def _():
        from_out[...] = jnp.zeros_like(from_out)

    @pl.loop(0, count)
    def _(c):
        span = pl.ds(pl.multiple_of(c * rows, rows), rows)
        ends[0:2] = from_in[:, span]
        ends[2:4] = from_out[:, span]
        rim = ends[0:4]
        rim_high = rim.astype(BF16).astype(F32)
        ends[0:4] = rim_high
        ends[4:8] = rim_high
        ends[8:12] = rim - rim_high
        high, low = halves(block[pl.ds(c * chunk, chunk)])
        both = dot(paired(high, low), rad_main_v[...])
        outside = lax.dot_general(
            ends[...].astype(BF16), rad_use_v[...], (((0,), (0,)), ((), ())),
            preferred_element_type=F32,
        )
        slope = (both[:, :cells_r] + both[:, cells_r:] + outside) * metric[...]
        grad_radial[pl.ds(c * chunk, chunk)] = slope.reshape(chunk, cells_t, cells_r)

    for pair in [raw_sends] + sum_sends:
        for copy in pair:
            copy.wait()


def stacked(high, low, p):
    return jnp.concatenate(
        [jnp.concatenate([high[q], high[q], low[q]], axis=0) for q in (p, p + 1)], axis=1
    )


def paired(high, low):
    planes, cells_t, cells_r = high.shape
    rows = planes * cells_t
    return jnp.concatenate([high.reshape(rows, cells_r), low.reshape(rows, cells_r)], axis=1)


def join_kernel(
    chunk, part_slope, part_smooth, radial, raw_left, raw_right, sum_left, sum_right,
    azi_use, azimuth_metric,
    grad_azimuth, filtered, grad_radial,
    slopes, smooths, rims, radial_sem, sems,
):
    planes, cells_t, cells_r = part_slope.shape
    count = planes // chunk
    groups = chunk // PACK
    radial_copy = pltpu.make_async_copy(radial, grad_radial, radial_sem)
    radial_copy.start()
    rims[...] = jnp.zeros_like(rims)

    def stores(c):
        span = pl.ds(c * chunk, chunk)
        return [
            pltpu.make_async_copy(source.at[span], target.at[span], sems.at[k, c])
            for k, (source, target) in enumerate(((slopes, grad_azimuth), (smooths, filtered)))
        ]

    @pl.loop(0, count)
    def _(c):
        for p in range(chunk):
            group, slot = divmod(p, PACK)
            span = slice(SUMS * slot, SUMS * (slot + 1))
            rims[p, 0:RAW, :] = raw_left[c * chunk + p]
            rims[p, RAW : 2 * RAW, :] = raw_right[c * chunk + p]
            rims[p, 8:10, :] = sum_left[c * groups + group, span, :]
            rims[p, 10:12, :] = sum_right[c * groups + group, span, :]
        high, low = halves(rims[...])
        for p in range(0, chunk, 2):
            result = dot(azi_use[...], stacked(high, low, p))
            for k in range(2):
                q = c * chunk + p + k
                lanes = slice(k * cells_r, (k + 1) * cells_r)
                slopes[q] = (part_slope[q] + result[:cells_t, lanes]) * azimuth_metric[...]
                smooths[q] = part_smooth[q] + result[cells_t:, lanes]
        for copy in stores(c):
            copy.start()

    @pl.loop(0, count)
    def _(c):
        for copy in stores(c):
            copy.wait()

    radial_copy.wait()


def local(tables, azi_count, rad_count, fields, radial_metric, azimuth_metric):
    azi_send, azi_main, azi_use, rad_send, rad_main, rad_use = [jnp.asarray(t) for t in tables]
    shape = fields.shape
    cells_t, cells_r = shape[2], shape[3]
    planes = shape[0] * shape[1]
    x = fields.reshape(planes, cells_t, cells_r)
    chunk = 8
    count = planes // chunk
    raws = jax.ShapeDtypeStruct((planes, RAW, cells_r), F32)
    sums = jax.ShapeDtypeStruct((planes // PACK, PACK * SUMS, cells_r), F32)
    full = jax.ShapeDtypeStruct(x.shape, F32)
    ends = pltpu.VMEM((2, planes * cells_t), F32)
    hbm = pl.BlockSpec(memory_space=pltpu.HBM)
    vmem = pl.BlockSpec(memory_space=pltpu.VMEM)
    dma = pltpu.SemaphoreType.DMA
    raw_left, raw_right, sum_left, sum_right, part_slope, part_smooth, radial = pl.pallas_call(
        functools.partial(block_kernel, azi_count, rad_count, chunk),
        out_shape=[raws, raws, sums, sums, full, full, full],
        in_specs=[hbm] * 7,
        out_specs=[vmem] * 7,
        scratch_shapes=[
            pltpu.VMEM(x.shape, F32),
            pltpu.VMEM(azi_send.shape, BF16),
            pltpu.VMEM(azi_main.shape, BF16),
            pltpu.VMEM(rad_send.shape[1:], BF16),
            pltpu.VMEM(rad_main.shape[1:], BF16),
            pltpu.VMEM(rad_use.shape[1:], BF16),
            pltpu.VMEM((1, cells_r), F32),
            pltpu.VMEM(sums.shape, F32),
            pltpu.VMEM(sums.shape, F32),
            ends,
            ends,
            ends,
            ends,
            pltpu.VMEM((16, chunk * cells_t), F32),
            dma((6,)),
            dma((count,)),
            dma((8,)),
            dma((8,)),
            dma((2,)),
            dma((2,)),
            pltpu.SemaphoreType.REGULAR((3,)),
        ],
        compiler_params=pltpu.CompilerParams(
            collective_id=0, has_side_effects=True, vmem_limit_bytes=24 * 2**20
        ),
    )(
        *[
            pltpu.with_memory_space_constraint(a, pltpu.HBM)
            for a in (x, azi_send, azi_main, rad_send, rad_main, rad_use, radial_metric.reshape(1, cells_r))
        ]
    )

    outs = pl.pallas_call(
        functools.partial(join_kernel, chunk),
        out_shape=[full] * 3,
        in_specs=[vmem] * 9,
        out_specs=[hbm] * 3,
        scratch_shapes=[
            pltpu.VMEM(x.shape, F32),
            pltpu.VMEM(x.shape, F32),
            pltpu.VMEM((chunk, 16, cells_r), F32),
            dma,
            dma((2, count)),
        ],
        compiler_params=pltpu.CompilerParams(vmem_limit_bytes=24 * 2**20),
    )(
        part_slope, part_smooth, radial, raw_left, raw_right, sum_left, sum_right, azi_use,
        azimuth_metric.reshape(1, cells_r),
    )
    grad_azimuth, filtered, grad_radial = [a.reshape(shape) for a in outs]
    return grad_azimuth, grad_radial, filtered


def solution(mesh):
    rad_count, azi_count = mesh.shape["rad"], mesh.shape["azi"]
    spec = P(None, None, "azi", "rad")

    def run(fields, radial_metric, azimuth_metric):
        tables = build_tables(
            fields.shape[2] // azi_count, azi_count, fields.shape[3] // rad_count, rad_count
        )
        body = functools.partial(local, tables, azi_count, rad_count)
        return jax.shard_map(
            body,
            mesh=mesh,
            in_specs=(spec, P("rad"), P("rad")),
            out_specs=(spec, spec, spec),
            check_vma=False,
        )(fields, radial_metric, azimuth_metric)

    return run
```

```python
import functools

import jax
import jax.numpy as jnp
import ml_dtypes
import numpy as np
from jax import lax
from jax.experimental import pallas as pl
from jax.experimental.pallas import tpu as pltpu
from jax.sharding import PartitionSpec as P

ALPHA_D = 1.0 / 3.0
COEF_A = 14.0 / 9.0
COEF_B = 1.0 / 9.0
ALPHA_F = 0.49
MESH = pl.DeviceIdType.MESH
BF16 = jnp.bfloat16
F32 = jnp.float32

RAW = 4
SUMS = 2
PACK = 4


def filter_weights():
    slack = 1.0 - 2.0 * ALPHA_F
    return [
        (193.0 + 126.0 * ALPHA_F) / 256.0,
        (105.0 + 302.0 * ALPHA_F) / 256.0,
        -15.0 * slack / 64.0,
        45.0 * slack / 512.0,
        -5.0 * slack / 256.0,
        slack / 512.0,
    ]


def split(table):
    table = np.asarray(table, np.float32)
    high = table.astype(ml_dtypes.bfloat16)
    low = (table - high.astype(np.float32)).astype(ml_dtypes.bfloat16)
    return high, low


def decay(alpha):
    return (-1.0 + np.sqrt(1.0 - 4.0 * alpha * alpha)) / (2.0 * alpha)


def azimuth_tables(cells, blocks):
    total = cells * blocks
    wave = 2.0 * np.pi * np.arange(total) / total
    slope_symbol = 1j * (COEF_A * np.sin(wave) + 0.5 * COEF_B * np.sin(2.0 * wave))
    slope_symbol = slope_symbol / (1.0 + 2.0 * ALPHA_D * np.cos(wave))
    weights = filter_weights()
    smooth_symbol = sum(w * np.cos(n * wave) for n, w in enumerate(weights))
    smooth_symbol = smooth_symbol / (1.0 + 2.0 * ALPHA_F * np.cos(wave))
    slope = np.real(np.fft.ifft(slope_symbol))
    smooth = np.real(np.fft.ifft(smooth_symbol))
    i = np.arange(cells)
    gap = (i[:, None] - i[None, :]) % total
    main = np.concatenate([slope[gap], smooth[gap]], axis=0)
    rate_d, rate_f = decay(ALPHA_D), decay(ALPHA_F)
    scale_d = slope[2] / rate_d**2
    scale_f = smooth[5] / rate_f**5
    send_right = np.stack([rate_d ** (cells - 1 - i), rate_f ** (cells - 1 - i)])
    sums = np.zeros((2 * cells, SUMS))
    sums[:cells, 0] = scale_d * rate_d ** (i + 1)
    sums[cells:, 1] = scale_f * rate_f ** (i + 1)
    raw = np.zeros((2 * cells, RAW))
    for m in range(RAW):
        for row in range(RAW - m):
            n = row + 1 + m
            if n < 2:
                raw[row, RAW - 1 - m] = slope[n] - scale_d * rate_d**n
            if n < 5:
                raw[cells + row, RAW - 1 - m] = smooth[n] - scale_f * rate_f**n
    send_left = send_right[:, ::-1]

    def mirrored(table):
        return np.concatenate([-table[:cells][::-1], table[cells:][::-1]], axis=0)

    uses = np.concatenate([raw, mirrored(raw)[:, ::-1], sums, mirrored(sums)], axis=1)
    return main, np.concatenate([send_right, send_left], axis=0), uses


def radial_matrix(total):
    system = np.eye(total) + ALPHA_D * (np.eye(total, k=1) + np.eye(total, k=-1))
    side = 0.5 * COEF_A * (np.eye(total, k=1) - np.eye(total, k=-1))
    side = side + 0.25 * COEF_B * (np.eye(total, k=2) - np.eye(total, k=-2))
    return np.linalg.solve(system, side)


def rank_two(corner):
    cells = corner.shape[0]
    send = np.zeros((2, cells))
    send[0] = corner[1] / corner[1, cells - 1]
    send[1, cells - 1] = 1.0
    use = np.zeros((cells, 2))
    use[1:, 0] = corner[1:, cells - 1]
    use[0, 0] = corner[0, cells - 2] / send[0, cells - 2]
    use[0, 1] = corner[0, cells - 1] - use[0, 0]
    return use, send


def radial_tables(cells, blocks):
    full = radial_matrix(cells * blocks).reshape(blocks, cells, blocks, cells)
    main = np.stack([full[b, :, b, :] for b in range(blocks)])
    use_left = np.zeros((blocks, cells, 2))
    use_right = np.zeros((blocks, cells, 2))
    send_right = np.zeros((blocks, 2, cells))
    send_left = np.zeros((blocks, 2, cells))
    for b in range(1, blocks):
        use_left[b], send_right[b - 1] = rank_two(full[b, :, b - 1, :])
    for b in range(blocks - 1):
        use, send = rank_two(full[b, :, b + 1, :][::-1, ::-1])
        use_right[b], send_left[b + 1] = use[::-1], send[:, ::-1]
    return main, send_right, send_left, use_left, use_right


def build_tables(cells_t, azi_count, cells_r, rad_count):
    main, edge_sums, edge_uses = azimuth_tables(cells_t, azi_count)
    azi_send = np.broadcast_to(edge_sums[:, :, None], edge_sums.shape + (cells_r,))
    azi_send = np.ascontiguousarray(azi_send, np.float32)
    uses = np.zeros((2 * cells_t, 16))
    uses[:, : edge_uses.shape[1]] = edge_uses
    high, low = split(main)
    use_high, use_low = split(uses)
    azi_main = np.concatenate([high, low, high], axis=1)
    azi_use = np.concatenate([use_high, use_low, use_high], axis=1)

    main, send_right, send_left, use_left, use_right = radial_tables(cells_r, rad_count)
    sends = np.concatenate([send_right, send_left], axis=1)
    high, low = split(sends)
    rad_send = np.zeros((rad_count, 16, 2 * cells_r), ml_dtypes.bfloat16)
    rad_send[:, 0:4, :cells_r] = high
    rad_send[:, 0:4, cells_r:] = high
    rad_send[:, 8:12, :cells_r] = low
    turned = np.swapaxes(main, 1, 2)
    high, low = split(turned)
    rad_main = np.zeros((rad_count, 2 * cells_r, 2 * cells_r), ml_dtypes.bfloat16)
    rad_main[:, :cells_r, :cells_r] = high
    rad_main[:, :cells_r, cells_r:] = low
    rad_main[:, cells_r:, :cells_r] = high
    uses = np.swapaxes(np.concatenate([use_left, use_right], axis=2), 1, 2)
    high, low = split(uses)
    rad_use = np.zeros((rad_count, 16, cells_r), ml_dtypes.bfloat16)
    rad_use[:, 0:4], rad_use[:, 4:8], rad_use[:, 8:12] = high, low, high
    return azi_send, azi_main, azi_use, rad_send, rad_main, rad_use


def halves(x):
    high = x.astype(BF16)
    return high, (x - high.astype(F32)).astype(BF16)


def dot(a, b):
    return jnp.dot(a, b, preferred_element_type=F32)


def block_kernel(
    azi_count, rad_count, chunk,
    fields, azi_send, azi_main, rad_send, rad_main, rad_use, radial_metric,
    raw_left, raw_right, sum_left, sum_right, part_slope, part_smooth, grad_radial,
    block, azi_send_v, azi_main_v, rad_send_v, rad_main_v, rad_use_v, metric,
    to_right, to_left, to_out, to_in, from_in, from_out, ends,
    table_sem, load_sem, send_sem, recv_sem, rad_send_sem, rad_recv_sem, ready,
):
    planes, cells_t, cells_r = block.shape
    count = planes // chunk
    rows = chunk * cells_t
    groups = chunk // PACK
    rad, azi = lax.axis_index("rad"), lax.axis_index("azi")
    right = (rad, lax.rem(azi + 1, azi_count))
    left = (rad, lax.rem(azi + azi_count - 1, azi_count))
    outer = (lax.rem(rad + 1, rad_count), azi)
    inner = (lax.rem(rad + rad_count - 1, rad_count), azi)
    has_outer, has_inner = rad < rad_count - 1, rad > 0
    is_first, is_last = azi == 0, azi == azi_count - 1
    last = azi_count - 1
    early = jnp.logical_and(lax.rem(azi, 2) == 1, azi != last - 2)
    tells_left = jnp.logical_and(lax.rem(azi, 2) == 0, jnp.logical_and(azi > 0, azi < last - 1))
    late = jnp.logical_not(early)
    even = lax.rem(rad, 2) == 0
    odd = jnp.logical_not(even)
    barrier = pltpu.get_barrier_semaphore()

    @pl.when(jnp.logical_not(tells_left))
    def _():
        pl.semaphore_signal(barrier, inc=1, device_id=left, device_id_type=MESH)

    @pl.when(azi < azi_count - 2)
    def _():
        pl.semaphore_signal(barrier, inc=1, device_id=right, device_id_type=MESH)

    @pl.when(jnp.logical_and(odd, has_outer))
    def _():
        pl.semaphore_signal(barrier, inc=1, device_id=outer, device_id_type=MESH)

    @pl.when(odd)
    def _():
        pl.semaphore_signal(barrier, inc=1, device_id=inner, device_id_type=MESH)

    def load(c):
        span = pl.ds(c * chunk, chunk)
        return pltpu.make_async_copy(fields.at[span], block.at[span], load_sem.at[c])

    tables = [
        pltpu.make_async_copy(source, target, table_sem.at[k])
        for k, (source, target) in enumerate(
            (
                (azi_send, azi_send_v),
                (rad_send.at[rad], rad_send_v),
                (azi_main, azi_main_v),
                (rad_main.at[rad], rad_main_v),
                (rad_use.at[rad], rad_use_v),
                (radial_metric, metric),
            )
        )
    ]

    def send(k, source, target, place):
        return pltpu.make_async_remote_copy(
            src_ref=source,
            dst_ref=target,
            send_sem=send_sem.at[k],
            recv_sem=recv_sem.at[k],
            device_id=place,
            device_id_type=MESH,
        )

    raw_sends = (
        send(0, fields.at[:, pl.ds(cells_t - RAW, RAW)], raw_left, right),
        send(1, fields.at[:, pl.ds(0, RAW)], raw_right, left),
    )
    cuts = [0, count - 2, count]

    def sums(part):
        span = pl.ds(cuts[part] * groups, (cuts[part + 1] - cuts[part]) * groups)
        return (
            send(2 + 2 * part, to_right.at[span], sum_left.at[span], right),
            send(3 + 2 * part, to_left.at[span], sum_right.at[span], left),
        )

    sum_sends = [sums(part) for part in range(len(cuts) - 1)]
    out_send, in_send = [
        pltpu.make_async_remote_copy(
            src_ref=source,
            dst_ref=target,
            send_sem=rad_send_sem.at[k],
            recv_sem=rad_recv_sem.at[k],
            device_id=place,
            device_id_type=MESH,
        )
        for k, (source, target, place) in enumerate(
            ((to_out, from_in, outer), (to_in, from_out, inner))
        )
    ]

    tables[0].start()
    for c in range(count):
        load(c).start()
    for table in tables[1:]:
        table.start()

    def first(pair):
        @pl.when(right_first)
        def _():
            pair[0].start()

        @pl.when(jnp.logical_not(right_first))
        def _():
            pair[1].start()

    def second(pair):
        @pl.when(right_first)
        def _():
            pair[1].start()

        @pl.when(jnp.logical_not(right_first))
        def _():
            pair[0].start()

    def early_first(pair):
        @pl.when(is_last)
        def _():
            pair[0].start()

        @pl.when(jnp.logical_and(early, jnp.logical_not(is_last)))
        def _():
            pair[1].start()

    def early_second(pair):
        @pl.when(is_last)
        def _():
            pair[1].start()

        @pl.when(jnp.logical_and(early, jnp.logical_not(is_last)))
        def _():
            pair[0].start()

    def greet():
        neighbours = jnp.where(jnp.logical_or(early, is_first), 1, 2)
        beside = has_inner.astype(jnp.int32) + has_outer.astype(jnp.int32)
        pl.semaphore_wait(barrier, neighbours + jnp.where(even, beside, 0))

        @pl.when(azi >= azi_count - 2)
        def _():
            pl.semaphore_signal(ready.at[0], inc=1, device_id=right, device_id_type=MESH)

        @pl.when(tells_left)
        def _():
            pl.semaphore_signal(ready.at[0], inc=1, device_id=left, device_id_type=MESH)

        @pl.when(jnp.logical_and(even, has_inner))
        def _():
            pl.semaphore_signal(ready.at[1], inc=1, device_id=inner, device_id_type=MESH)

        @pl.when(jnp.logical_and(even, has_outer))
        def _():
            pl.semaphore_signal(ready.at[2], inc=1, device_id=outer, device_id_type=MESH)

    @pl.when(early)
    def _():
        greet()

    early_first(raw_sends)
    tables[0].wait()

    def edges(c):
        load(c).wait()
        for p in range(chunk):
            plane = block[c * chunk + p]
            group, slot = divmod(p, PACK)
            span = slice(SUMS * slot, SUMS * (slot + 1))
            both = [
                jnp.sum(plane * azi_send_v[k], axis=0, keepdims=True) for k in range(2 * SUMS)
            ]
            to_right[c * groups + group, span, :] = jnp.concatenate(both[:SUMS], axis=0)
            to_left[c * groups + group, span, :] = jnp.concatenate(both[SUMS:], axis=0)

    for part in range(len(cuts) - 1):
        pl.loop(cuts[part], cuts[part + 1])(edges)
        early_first(sum_sends[part])

    @pl.when(late)
    def _():
        greet()

        @pl.when(jnp.logical_not(is_first))
        def _():
            raw_sends[1].start()
            for pair in sum_sends:
                pair[1].start()

        raw_sends[0].start()
        for pair in sum_sends:
            pair[0].start()

    tables[1].wait()

    @pl.loop(0, count)
    def _(c):
        high, low = halves(block[pl.ds(c * chunk, chunk)])
        tips = lax.dot_general(
            rad_send_v[...], paired(high, low), (((1,), (1,)), ((), ())),
            preferred_element_type=F32,
        )
        tips = tips[0:8] + tips[8:16]
        span = pl.ds(pl.multiple_of(c * rows, rows), rows)
        to_out[:, span] = tips[0:2]
        to_in[:, span] = tips[2:4]

    @pl.when(jnp.logical_and(even, has_inner))
    def _():
        in_send.start()

    @pl.when(jnp.logical_and(even, has_outer))
    def _():
        out_send.start()

    @pl.when(early)
    def _():
        pl.semaphore_wait(ready.at[0], 1)

    early_second(raw_sends)
    for pair in sum_sends:
        early_second(pair)

    for table in tables[2:]:
        table.wait()
    ends[...] = jnp.zeros_like(ends)

    @pl.loop(0, count)
    def _(c):
        high, low = halves(block[pl.ds(c * chunk, chunk)])
        for p in range(0, chunk, 2):
            result = dot(azi_main_v[...], stacked(high, low, p))
            for k in range(2):
                lanes = slice(k * cells_r, (k + 1) * cells_r)
                part_slope[c * chunk + p + k] = result[:cells_t, lanes]
                part_smooth[c * chunk + p + k] = result[cells_t:, lanes]

    @pl.when(is_first)
    def _():
        pl.semaphore_wait(ready.at[0], 1)
        raw_sends[1].start()
        for pair in sum_sends:
            pair[1].start()

    @pl.when(odd)
    def _():
        pl.semaphore_wait(ready.at[2], 1)
        in_send.start()

    @pl.when(jnp.logical_and(odd, has_outer))
    def _():
        pl.semaphore_wait(ready.at[1], 1)
        out_send.start()

    @pl.when(has_inner)
    def _():
        in_send.wait_send()
        out_send.wait_recv()

    @pl.when(jnp.logical_not(has_inner))
    def _():
        from_in[...] = jnp.zeros_like(from_in)

    @pl.when(has_outer)
    def _():
        out_send.wait_send()
        in_send.wait_recv()

    @pl.when(jnp.logical_not(has_outer))
    def _():
        from_out[...] = jnp.zeros_like(from_out)

    @pl.loop(0, count)
    def _(c):
        span = pl.ds(pl.multiple_of(c * rows, rows), rows)
        ends[0:2] = from_in[:, span]
        ends[2:4] = from_out[:, span]
        rim = ends[0:4]
        rim_high = rim.astype(BF16).astype(F32)
        ends[0:4] = rim_high
        ends[4:8] = rim_high
        ends[8:12] = rim - rim_high
        high, low = halves(block[pl.ds(c * chunk, chunk)])
        both = dot(paired(high, low), rad_main_v[...])
        outside = lax.dot_general(
            ends[...].astype(BF16), rad_use_v[...], (((0,), (0,)), ((), ())),
            preferred_element_type=F32,
        )
        slope = (both[:, :cells_r] + both[:, cells_r:] + outside) * metric[...]
        grad_radial[pl.ds(c * chunk, chunk)] = slope.reshape(chunk, cells_t, cells_r)

    for pair in [raw_sends] + sum_sends:
        for copy in pair:
            copy.wait()


def stacked(high, low, p):
    return jnp.concatenate(
        [jnp.concatenate([high[q], high[q], low[q]], axis=0) for q in (p, p + 1)], axis=1
    )


def paired(high, low):
    planes, cells_t, cells_r = high.shape
    rows = planes * cells_t
    return jnp.concatenate([high.reshape(rows, cells_r), low.reshape(rows, cells_r)], axis=1)


def join_kernel(
    chunk, part_slope, part_smooth, radial, raw_left, raw_right, sum_left, sum_right,
    azi_use, azimuth_metric,
    grad_azimuth, filtered, grad_radial,
    slopes, smooths, rims, radial_sem, sems,
):
    planes, cells_t, cells_r = part_slope.shape
    count = planes // chunk
    groups = chunk // PACK
    radial_copy = pltpu.make_async_copy(radial, grad_radial, radial_sem)
    radial_copy.start()
    rims[...] = jnp.zeros_like(rims)

    def stores(c):
        span = pl.ds(c * chunk, chunk)
        return [
            pltpu.make_async_copy(source.at[span], target.at[span], sems.at[k, c])
            for k, (source, target) in enumerate(((slopes, grad_azimuth), (smooths, filtered)))
        ]

    @pl.loop(0, count)
    def _(c):
        for p in range(chunk):
            group, slot = divmod(p, PACK)
            span = slice(SUMS * slot, SUMS * (slot + 1))
            rims[p, 0:RAW, :] = raw_left[c * chunk + p]
            rims[p, RAW : 2 * RAW, :] = raw_right[c * chunk + p]
            rims[p, 8:10, :] = sum_left[c * groups + group, span, :]
            rims[p, 10:12, :] = sum_right[c * groups + group, span, :]
        high, low = halves(rims[...])
        for p in range(0, chunk, 2):
            result = dot(azi_use[...], stacked(high, low, p))
            for k in range(2):
                q = c * chunk + p + k
                lanes = slice(k * cells_r, (k + 1) * cells_r)
                slopes[q] = (part_slope[q] + result[:cells_t, lanes]) * azimuth_metric[...]
                smooths[q] = part_smooth[q] + result[cells_t:, lanes]
        for copy in stores(c):
            copy.start()

    @pl.loop(0, count)
    def _(c):
        for copy in stores(c):
            copy.wait()

    radial_copy.wait()


def local(tables, azi_count, rad_count, fields, radial_metric, azimuth_metric):
    azi_send, azi_main, azi_use, rad_send, rad_main, rad_use = [jnp.asarray(t) for t in tables]
    shape = fields.shape
    cells_t, cells_r = shape[2], shape[3]
    planes = shape[0] * shape[1]
    x = fields.reshape(planes, cells_t, cells_r)
    chunk = 8
    count = planes // chunk
    raws = jax.ShapeDtypeStruct((planes, RAW, cells_r), F32)
    sums = jax.ShapeDtypeStruct((planes // PACK, PACK * SUMS, cells_r), F32)
    full = jax.ShapeDtypeStruct(x.shape, F32)
    ends = pltpu.VMEM((2, planes * cells_t), F32)
    hbm = pl.BlockSpec(memory_space=pltpu.HBM)
    vmem = pl.BlockSpec(memory_space=pltpu.VMEM)
    dma = pltpu.SemaphoreType.DMA
    raw_left, raw_right, sum_left, sum_right, part_slope, part_smooth, radial = pl.pallas_call(
        functools.partial(block_kernel, azi_count, rad_count, chunk),
        out_shape=[raws, raws, sums, sums, full, full, full],
        in_specs=[hbm] * 7,
        out_specs=[vmem] * 7,
        scratch_shapes=[
            pltpu.VMEM(x.shape, F32),
            pltpu.VMEM(azi_send.shape, F32),
            pltpu.VMEM(azi_main.shape, BF16),
            pltpu.VMEM(rad_send.shape[1:], BF16),
            pltpu.VMEM(rad_main.shape[1:], BF16),
            pltpu.VMEM(rad_use.shape[1:], BF16),
            pltpu.VMEM((1, cells_r), F32),
            pltpu.VMEM(sums.shape, F32),
            pltpu.VMEM(sums.shape, F32),
            ends,
            ends,
            ends,
            ends,
            pltpu.VMEM((16, chunk * cells_t), F32),
            dma((6,)),
            dma((count,)),
            dma((8,)),
            dma((8,)),
            dma((2,)),
            dma((2,)),
            pltpu.SemaphoreType.REGULAR((3,)),
        ],
        compiler_params=pltpu.CompilerParams(
            collective_id=0, has_side_effects=True, vmem_limit_bytes=24 * 2**20
        ),
    )(
        *[
            pltpu.with_memory_space_constraint(a, pltpu.HBM)
            for a in (x, azi_send, azi_main, rad_send, rad_main, rad_use, radial_metric.reshape(1, cells_r))
        ]
    )

    outs = pl.pallas_call(
        functools.partial(join_kernel, chunk),
        out_shape=[full] * 3,
        in_specs=[vmem] * 9,
        out_specs=[hbm] * 3,
        scratch_shapes=[
            pltpu.VMEM(x.shape, F32),
            pltpu.VMEM(x.shape, F32),
            pltpu.VMEM((chunk, 16, cells_r), F32),
            dma,
            dma((2, count)),
        ],
        compiler_params=pltpu.CompilerParams(vmem_limit_bytes=24 * 2**20),
    )(
        part_slope, part_smooth, radial, raw_left, raw_right, sum_left, sum_right, azi_use,
        azimuth_metric.reshape(1, cells_r),
    )
    grad_azimuth, filtered, grad_radial = [a.reshape(shape) for a in outs]
    return grad_azimuth, grad_radial, filtered


def solution(mesh):
    rad_count, azi_count = mesh.shape["rad"], mesh.shape["azi"]
    spec = P(None, None, "azi", "rad")

    def run(fields, radial_metric, azimuth_metric):
        tables = build_tables(
            fields.shape[2] // azi_count, azi_count, fields.shape[3] // rad_count, rad_count
        )
        body = functools.partial(local, tables, azi_count, rad_count)
        return jax.shard_map(
            body,
            mesh=mesh,
            in_specs=(spec, P("rad"), P("rad")),
            out_specs=(spec, spec, spec),
            check_vma=False,
        )(fields, radial_metric, azimuth_metric)

    return run
```

```python
import functools

import jax
import jax.numpy as jnp
import ml_dtypes
import numpy as np
from jax import lax
from jax.experimental import pallas as pl
from jax.experimental.pallas import tpu as pltpu
from jax.sharding import PartitionSpec as P

ALPHA_D = 1.0 / 3.0
COEF_A = 14.0 / 9.0
COEF_B = 1.0 / 9.0
ALPHA_F = 0.49
MESH = pl.DeviceIdType.MESH
BF16 = jnp.bfloat16
F32 = jnp.float32

RAW = 4
SUMS = 2
PACK = 4


def filter_weights():
    slack = 1.0 - 2.0 * ALPHA_F
    return [
        (193.0 + 126.0 * ALPHA_F) / 256.0,
        (105.0 + 302.0 * ALPHA_F) / 256.0,
        -15.0 * slack / 64.0,
        45.0 * slack / 512.0,
        -5.0 * slack / 256.0,
        slack / 512.0,
    ]


def split(table):
    table = np.asarray(table, np.float32)
    high = table.astype(ml_dtypes.bfloat16)
    low = (table - high.astype(np.float32)).astype(ml_dtypes.bfloat16)
    return high, low


def decay(alpha):
    return (-1.0 + np.sqrt(1.0 - 4.0 * alpha * alpha)) / (2.0 * alpha)


def azimuth_tables(cells, blocks):
    total = cells * blocks
    wave = 2.0 * np.pi * np.arange(total) / total
    slope_symbol = 1j * (COEF_A * np.sin(wave) + 0.5 * COEF_B * np.sin(2.0 * wave))
    slope_symbol = slope_symbol / (1.0 + 2.0 * ALPHA_D * np.cos(wave))
    weights = filter_weights()
    smooth_symbol = sum(w * np.cos(n * wave) for n, w in enumerate(weights))
    smooth_symbol = smooth_symbol / (1.0 + 2.0 * ALPHA_F * np.cos(wave))
    slope = np.real(np.fft.ifft(slope_symbol))
    smooth = np.real(np.fft.ifft(smooth_symbol))
    i = np.arange(cells)
    gap = (i[:, None] - i[None, :]) % total
    main = np.concatenate([slope[gap], smooth[gap]], axis=0)
    rate_d, rate_f = decay(ALPHA_D), decay(ALPHA_F)
    scale_d = slope[2] / rate_d**2
    scale_f = smooth[5] / rate_f**5
    send_right = np.stack([rate_d ** (cells - 1 - i), rate_f ** (cells - 1 - i)])
    sums = np.zeros((2 * cells, SUMS))
    sums[:cells, 0] = scale_d * rate_d ** (i + 1)
    sums[cells:, 1] = scale_f * rate_f ** (i + 1)
    raw = np.zeros((2 * cells, RAW))
    for m in range(RAW):
        for row in range(RAW - m):
            n = row + 1 + m
            if n < 2:
                raw[row, RAW - 1 - m] = slope[n] - scale_d * rate_d**n
            if n < 5:
                raw[cells + row, RAW - 1 - m] = smooth[n] - scale_f * rate_f**n
    send_left = send_right[:, ::-1]

    def mirrored(table):
        return np.concatenate([-table[:cells][::-1], table[cells:][::-1]], axis=0)

    uses = np.concatenate([raw, mirrored(raw)[:, ::-1], sums, mirrored(sums)], axis=1)
    return main, np.concatenate([send_right, send_left], axis=0), uses


def radial_matrix(total):
    system = np.eye(total) + ALPHA_D * (np.eye(total, k=1) + np.eye(total, k=-1))
    side = 0.5 * COEF_A * (np.eye(total, k=1) - np.eye(total, k=-1))
    side = side + 0.25 * COEF_B * (np.eye(total, k=2) - np.eye(total, k=-2))
    return np.linalg.solve(system, side)


def rank_two(corner):
    cells = corner.shape[0]
    send = np.zeros((2, cells))
    send[0] = corner[1] / corner[1, cells - 1]
    send[1, cells - 1] = 1.0
    use = np.zeros((cells, 2))
    use[1:, 0] = corner[1:, cells - 1]
    use[0, 0] = corner[0, cells - 2] / send[0, cells - 2]
    use[0, 1] = corner[0, cells - 1] - use[0, 0]
    return use, send


def radial_tables(cells, blocks):
    full = radial_matrix(cells * blocks).reshape(blocks, cells, blocks, cells)
    main = np.stack([full[b, :, b, :] for b in range(blocks)])
    use_left = np.zeros((blocks, cells, 2))
    use_right = np.zeros((blocks, cells, 2))
    send_right = np.zeros((blocks, 2, cells))
    send_left = np.zeros((blocks, 2, cells))
    for b in range(1, blocks):
        use_left[b], send_right[b - 1] = rank_two(full[b, :, b - 1, :])
    for b in range(blocks - 1):
        use, send = rank_two(full[b, :, b + 1, :][::-1, ::-1])
        use_right[b], send_left[b + 1] = use[::-1], send[:, ::-1]
    return main, send_right, send_left, use_left, use_right


def build_tables(cells_t, azi_count, cells_r, rad_count):
    main, edge_sums, edge_uses = azimuth_tables(cells_t, azi_count)
    azi_send = np.broadcast_to(edge_sums[:, :, None], edge_sums.shape + (cells_r,))
    azi_send = np.ascontiguousarray(azi_send, np.float32)
    uses = np.zeros((2 * cells_t, 16))
    uses[:, : edge_uses.shape[1]] = edge_uses
    high, low = split(main)
    use_high, use_low = split(uses)
    azi_main = np.concatenate([high, low, high], axis=1)
    azi_use = np.concatenate([use_high, use_low, use_high], axis=1)

    main, send_right, send_left, use_left, use_right = radial_tables(cells_r, rad_count)
    sends = np.concatenate([send_right, send_left], axis=1)
    high, low = split(sends)
    rad_send = np.zeros((rad_count, 16, 2 * cells_r), ml_dtypes.bfloat16)
    rad_send[:, 0:4, :cells_r] = high
    rad_send[:, 0:4, cells_r:] = high
    rad_send[:, 8:12, :cells_r] = low
    turned = np.swapaxes(main, 1, 2)
    high, low = split(turned)
    rad_main = np.zeros((rad_count, 2 * cells_r, 2 * cells_r), ml_dtypes.bfloat16)
    rad_main[:, :cells_r, :cells_r] = high
    rad_main[:, :cells_r, cells_r:] = low
    rad_main[:, cells_r:, :cells_r] = high
    uses = np.swapaxes(np.concatenate([use_left, use_right], axis=2), 1, 2)
    high, low = split(uses)
    rad_use = np.zeros((rad_count, 16, cells_r), ml_dtypes.bfloat16)
    rad_use[:, 0:4], rad_use[:, 4:8], rad_use[:, 8:12] = high, low, high
    return azi_send, azi_main, azi_use, rad_send, rad_main, rad_use


def halves(x):
    high = x.astype(BF16)
    return high, (x - high.astype(F32)).astype(BF16)


def dot(a, b):
    return jnp.dot(a, b, preferred_element_type=F32)


def block_kernel(
    azi_count, rad_count, chunk,
    fields, azi_send, azi_main, rad_send, rad_main, rad_use, radial_metric,
    raw_left, raw_right, sum_left, sum_right, part_slope, part_smooth, grad_radial,
    block, azi_send_v, azi_main_v, rad_send_v, rad_main_v, rad_use_v, metric,
    to_right, to_left, to_out, to_in, from_in, from_out, ends,
    table_sem, load_sem, send_sem, recv_sem, rad_send_sem, rad_recv_sem, ready,
):
    planes, cells_t, cells_r = block.shape
    count = planes // chunk
    rows = chunk * cells_t
    groups = chunk // PACK
    rad, azi = lax.axis_index("rad"), lax.axis_index("azi")
    right = (rad, lax.rem(azi + 1, azi_count))
    left = (rad, lax.rem(azi + azi_count - 1, azi_count))
    outer = (lax.rem(rad + 1, rad_count), azi)
    inner = (lax.rem(rad + rad_count - 1, rad_count), azi)
    has_outer, has_inner = rad < rad_count - 1, rad > 0
    is_first, is_last = azi == 0, azi == azi_count - 1
    last = azi_count - 1
    early = jnp.logical_and(lax.rem(azi, 2) == 1, azi != last - 2)
    tells_left = jnp.logical_and(lax.rem(azi, 2) == 0, jnp.logical_and(azi > 0, azi < last - 1))
    late = jnp.logical_not(early)
    even = lax.rem(rad, 2) == 0
    odd = jnp.logical_not(even)
    barrier = pltpu.get_barrier_semaphore()

    @pl.when(jnp.logical_not(tells_left))
    def _():
        pl.semaphore_signal(barrier, inc=1, device_id=left, device_id_type=MESH)

    @pl.when(azi < azi_count - 2)
    def _():
        pl.semaphore_signal(barrier, inc=1, device_id=right, device_id_type=MESH)

    @pl.when(jnp.logical_and(odd, has_outer))
    def _():
        pl.semaphore_signal(barrier, inc=1, device_id=outer, device_id_type=MESH)

    @pl.when(odd)
    def _():
        pl.semaphore_signal(barrier, inc=1, device_id=inner, device_id_type=MESH)

    def load(c):
        span = pl.ds(c * chunk, chunk)
        return pltpu.make_async_copy(fields.at[span], block.at[span], load_sem.at[c])

    tables = [
        pltpu.make_async_copy(source, target, table_sem.at[k])
        for k, (source, target) in enumerate(
            (
                (azi_send, azi_send_v),
                (rad_send.at[rad], rad_send_v),
                (azi_main, azi_main_v),
                (rad_main.at[rad], rad_main_v),
                (rad_use.at[rad], rad_use_v),
                (radial_metric, metric),
            )
        )
    ]

    def send(k, source, target, place):
        return pltpu.make_async_remote_copy(
            src_ref=source,
            dst_ref=target,
            send_sem=send_sem.at[k],
            recv_sem=recv_sem.at[k],
            device_id=place,
            device_id_type=MESH,
        )

    raw_sends = (
        send(0, fields.at[:, pl.ds(cells_t - RAW, RAW)], raw_left, right),
        send(1, fields.at[:, pl.ds(0, RAW)], raw_right, left),
    )
    cuts = [0, count - 1, count]

    def sums(part):
        span = pl.ds(cuts[part] * groups, (cuts[part + 1] - cuts[part]) * groups)
        return (
            send(2 + 2 * part, to_right.at[span], sum_left.at[span], right),
            send(3 + 2 * part, to_left.at[span], sum_right.at[span], left),
        )

    sum_sends = [sums(part) for part in range(len(cuts) - 1)]
    out_send, in_send = [
        pltpu.make_async_remote_copy(
            src_ref=source,
            dst_ref=target,
            send_sem=rad_send_sem.at[k],
            recv_sem=rad_recv_sem.at[k],
            device_id=place,
            device_id_type=MESH,
        )
        for k, (source, target, place) in enumerate(
            ((to_out, from_in, outer), (to_in, from_out, inner))
        )
    ]

    def first(pair):
        @pl.when(right_first)
        def _():
            pair[0].start()

        @pl.when(jnp.logical_not(right_first))
        def _():
            pair[1].start()

    def second(pair):
        @pl.when(right_first)
        def _():
            pair[1].start()

        @pl.when(jnp.logical_not(right_first))
        def _():
            pair[0].start()

    def early_first(pair):
        @pl.when(is_last)
        def _():
            pair[0].start()

        @pl.when(jnp.logical_and(early, jnp.logical_not(is_last)))
        def _():
            pair[1].start()

    def early_second(pair):
        @pl.when(is_last)
        def _():
            pair[1].start()

        @pl.when(jnp.logical_and(early, jnp.logical_not(is_last)))
        def _():
            pair[0].start()

    def greet():
        neighbours = jnp.where(jnp.logical_or(early, is_first), 1, 2)
        beside = has_inner.astype(jnp.int32) + has_outer.astype(jnp.int32)
        pl.semaphore_wait(barrier, neighbours + jnp.where(even, beside, 0))

        @pl.when(azi >= azi_count - 2)
        def _():
            pl.semaphore_signal(ready.at[0], inc=1, device_id=right, device_id_type=MESH)

        @pl.when(tells_left)
        def _():
            pl.semaphore_signal(ready.at[0], inc=1, device_id=left, device_id_type=MESH)

        @pl.when(jnp.logical_and(even, has_inner))
        def _():
            pl.semaphore_signal(ready.at[1], inc=1, device_id=inner, device_id_type=MESH)

        @pl.when(jnp.logical_and(even, has_outer))
        def _():
            pl.semaphore_signal(ready.at[2], inc=1, device_id=outer, device_id_type=MESH)

    @pl.when(is_last)
    def _():
        greet()
        raw_sends[0].start()

    tables[0].start()
    for c in range(count):
        load(c).start()
    for table in tables[1:]:
        table.start()

    @pl.when(jnp.logical_and(early, jnp.logical_not(is_last)))
    def _():
        greet()
        raw_sends[1].start()

    tables[0].wait()

    def edges(c):
        load(c).wait()
        for p in range(chunk):
            plane = block[c * chunk + p]
            group, slot = divmod(p, PACK)
            span = slice(SUMS * slot, SUMS * (slot + 1))
            both = [
                jnp.sum(plane * azi_send_v[k], axis=0, keepdims=True) for k in range(2 * SUMS)
            ]
            to_right[c * groups + group, span, :] = jnp.concatenate(both[:SUMS], axis=0)
            to_left[c * groups + group, span, :] = jnp.concatenate(both[SUMS:], axis=0)

    for part in range(len(cuts) - 1):
        pl.loop(cuts[part], cuts[part + 1])(edges)
        early_first(sum_sends[part])

    @pl.when(late)
    def _():
        greet()

        @pl.when(jnp.logical_not(is_first))
        def _():
            raw_sends[1].start()
            for pair in sum_sends:
                pair[1].start()

        raw_sends[0].start()
        for pair in sum_sends:
            pair[0].start()

    tables[1].wait()

    @pl.loop(0, count)
    def _(c):
        high, low = halves(block[pl.ds(c * chunk, chunk)])
        tips = lax.dot_general(
            rad_send_v[...], paired(high, low), (((1,), (1,)), ((), ())),
            preferred_element_type=F32,
        )
        tips = tips[0:8] + tips[8:16]
        span = pl.ds(pl.multiple_of(c * rows, rows), rows)
        to_out[:, span] = tips[0:2]
        to_in[:, span] = tips[2:4]

    @pl.when(jnp.logical_and(even, has_inner))
    def _():
        in_send.start()

    @pl.when(jnp.logical_and(even, has_outer))
    def _():
        out_send.start()

    @pl.when(early)
    def _():
        pl.semaphore_wait(ready.at[0], 1)

    early_second(raw_sends)
    for pair in sum_sends:
        early_second(pair)

    for table in tables[2:]:
        table.wait()
    ends[...] = jnp.zeros_like(ends)

    @pl.loop(0, count)
    def _(c):
        high, low = halves(block[pl.ds(c * chunk, chunk)])
        for p in range(0, chunk, 2):
            result = dot(azi_main_v[...], stacked(high, low, p))
            for k in range(2):
                lanes = slice(k * cells_r, (k + 1) * cells_r)
                part_slope[c * chunk + p + k] = result[:cells_t, lanes]
                part_smooth[c * chunk + p + k] = result[cells_t:, lanes]

    @pl.when(is_first)
    def _():
        pl.semaphore_wait(ready.at[0], 1)
        raw_sends[1].start()
        for pair in sum_sends:
            pair[1].start()

    @pl.when(odd)
    def _():
        pl.semaphore_wait(ready.at[2], 1)
        in_send.start()

    @pl.when(jnp.logical_and(odd, has_outer))
    def _():
        pl.semaphore_wait(ready.at[1], 1)
        out_send.start()

    @pl.when(has_inner)
    def _():
        in_send.wait_send()
        out_send.wait_recv()

    @pl.when(jnp.logical_not(has_inner))
    def _():
        from_in[...] = jnp.zeros_like(from_in)

    @pl.when(has_outer)
    def _():
        out_send.wait_send()
        in_send.wait_recv()

    @pl.when(jnp.logical_not(has_outer))
    def _():
        from_out[...] = jnp.zeros_like(from_out)

    @pl.loop(0, count)
    def _(c):
        span = pl.ds(pl.multiple_of(c * rows, rows), rows)
        ends[0:2] = from_in[:, span]
        ends[2:4] = from_out[:, span]
        rim = ends[0:4]
        rim_high = rim.astype(BF16).astype(F32)
        ends[0:4] = rim_high
        ends[4:8] = rim_high
        ends[8:12] = rim - rim_high
        high, low = halves(block[pl.ds(c * chunk, chunk)])
        both = dot(paired(high, low), rad_main_v[...])
        outside = lax.dot_general(
            ends[...].astype(BF16), rad_use_v[...], (((0,), (0,)), ((), ())),
            preferred_element_type=F32,
        )
        slope = (both[:, :cells_r] + both[:, cells_r:] + outside) * metric[...]
        grad_radial[pl.ds(c * chunk, chunk)] = slope.reshape(chunk, cells_t, cells_r)

    for pair in [raw_sends] + sum_sends:
        for copy in pair:
            copy.wait()


def stacked(high, low, p):
    return jnp.concatenate(
        [jnp.concatenate([high[q], high[q], low[q]], axis=0) for q in (p, p + 1)], axis=1
    )


def paired(high, low):
    planes, cells_t, cells_r = high.shape
    rows = planes * cells_t
    return jnp.concatenate([high.reshape(rows, cells_r), low.reshape(rows, cells_r)], axis=1)


def join_kernel(
    chunk, part_slope, part_smooth, radial, raw_left, raw_right, sum_left, sum_right,
    azi_use, azimuth_metric,
    grad_azimuth, filtered, grad_radial,
    slopes, smooths, rims, radial_sem, sems,
):
    planes, cells_t, cells_r = part_slope.shape
    count = planes // chunk
    groups = chunk // PACK
    radial_copy = pltpu.make_async_copy(radial, grad_radial, radial_sem)
    radial_copy.start()
    rims[...] = jnp.zeros_like(rims)

    def stores(c):
        span = pl.ds(c * chunk, chunk)
        return [
            pltpu.make_async_copy(source.at[span], target.at[span], sems.at[k, c])
            for k, (source, target) in enumerate(((slopes, grad_azimuth), (smooths, filtered)))
        ]

    @pl.loop(0, count)
    def _(c):
        for p in range(chunk):
            group, slot = divmod(p, PACK)
            span = slice(SUMS * slot, SUMS * (slot + 1))
            rims[p, 0:RAW, :] = raw_left[c * chunk + p]
            rims[p, RAW : 2 * RAW, :] = raw_right[c * chunk + p]
            rims[p, 8:10, :] = sum_left[c * groups + group, span, :]
            rims[p, 10:12, :] = sum_right[c * groups + group, span, :]
        high, low = halves(rims[...])
        for p in range(0, chunk, 2):
            result = dot(azi_use[...], stacked(high, low, p))
            for k in range(2):
                q = c * chunk + p + k
                lanes = slice(k * cells_r, (k + 1) * cells_r)
                slopes[q] = (part_slope[q] + result[:cells_t, lanes]) * azimuth_metric[...]
                smooths[q] = part_smooth[q] + result[cells_t:, lanes]
        for copy in stores(c):
            copy.start()

    @pl.loop(0, count)
    def _(c):
        for copy in stores(c):
            copy.wait()

    radial_copy.wait()


def local(tables, azi_count, rad_count, fields, radial_metric, azimuth_metric):
    azi_send, azi_main, azi_use, rad_send, rad_main, rad_use = [jnp.asarray(t) for t in tables]
    shape = fields.shape
    cells_t, cells_r = shape[2], shape[3]
    planes = shape[0] * shape[1]
    x = fields.reshape(planes, cells_t, cells_r)
    chunk = 8
    count = planes // chunk
    raws = jax.ShapeDtypeStruct((planes, RAW, cells_r), F32)
    sums = jax.ShapeDtypeStruct((planes // PACK, PACK * SUMS, cells_r), F32)
    full = jax.ShapeDtypeStruct(x.shape, F32)
    ends = pltpu.VMEM((2, planes * cells_t), F32)
    hbm = pl.BlockSpec(memory_space=pltpu.HBM)
    vmem = pl.BlockSpec(memory_space=pltpu.VMEM)
    dma = pltpu.SemaphoreType.DMA
    raw_left, raw_right, sum_left, sum_right, part_slope, part_smooth, radial = pl.pallas_call(
        functools.partial(block_kernel, azi_count, rad_count, chunk),
        out_shape=[raws, raws, sums, sums, full, full, full],
        in_specs=[hbm] * 7,
        out_specs=[vmem] * 7,
        scratch_shapes=[
            pltpu.VMEM(x.shape, F32),
            pltpu.VMEM(azi_send.shape, F32),
            pltpu.VMEM(azi_main.shape, BF16),
            pltpu.VMEM(rad_send.shape[1:], BF16),
            pltpu.VMEM(rad_main.shape[1:], BF16),
            pltpu.VMEM(rad_use.shape[1:], BF16),
            pltpu.VMEM((1, cells_r), F32),
            pltpu.VMEM(sums.shape, F32),
            pltpu.VMEM(sums.shape, F32),
            ends,
            ends,
            ends,
            ends,
            pltpu.VMEM((16, chunk * cells_t), F32),
            dma((6,)),
            dma((count,)),
            dma((8,)),
            dma((8,)),
            dma((2,)),
            dma((2,)),
            pltpu.SemaphoreType.REGULAR((3,)),
        ],
        compiler_params=pltpu.CompilerParams(
            collective_id=0, has_side_effects=True, vmem_limit_bytes=24 * 2**20
        ),
    )(
        *[
            pltpu.with_memory_space_constraint(a, pltpu.HBM)
            for a in (x, azi_send, azi_main, rad_send, rad_main, rad_use, radial_metric.reshape(1, cells_r))
        ]
    )

    outs = pl.pallas_call(
        functools.partial(join_kernel, chunk),
        out_shape=[full] * 3,
        in_specs=[vmem] * 9,
        out_specs=[hbm] * 3,
        scratch_shapes=[
            pltpu.VMEM(x.shape, F32),
            pltpu.VMEM(x.shape, F32),
            pltpu.VMEM((chunk, 16, cells_r), F32),
            dma,
            dma((2, count)),
        ],
        compiler_params=pltpu.CompilerParams(vmem_limit_bytes=24 * 2**20),
    )(
        part_slope, part_smooth, radial, raw_left, raw_right, sum_left, sum_right, azi_use,
        azimuth_metric.reshape(1, cells_r),
    )
    grad_azimuth, filtered, grad_radial = [a.reshape(shape) for a in outs]
    return grad_azimuth, grad_radial, filtered


def solution(mesh):
    rad_count, azi_count = mesh.shape["rad"], mesh.shape["azi"]
    spec = P(None, None, "azi", "rad")

    def run(fields, radial_metric, azimuth_metric):
        tables = build_tables(
            fields.shape[2] // azi_count, azi_count, fields.shape[3] // rad_count, rad_count
        )
        body = functools.partial(local, tables, azi_count, rad_count)
        return jax.shard_map(
            body,
            mesh=mesh,
            in_specs=(spec, P("rad"), P("rad")),
            out_specs=(spec, spec, spec),
            check_vma=False,
        )(fields, radial_metric, azimuth_metric)

    return run
```
